32 devices in a mesh: ctx: 16 (over z, x, core), ch: 2 (over y).
Axes of the slice: x: 2, y: 2, z: 4, core: 2. Of those that a mesh axis runs over, the one named last changes fastest.
Arguments:
- qkv: bfloat16 [3, 8192, 4096], P(None, 'ctx', 'ch'), may hold values from -6 to 6
- short_filter: float32 [3, 3, 4096], P(None, None, 'ch'), may hold values from -3 to 3
- long_filter: bfloat16 [2048, 4096], P(None, 'ch'), may hold values from -0.125 to 0.125
- skip: float32 [4096], P('ch'), may hold values from -1 to 1
- shard_doc: int32 [16], replicated, may hold values from 0 to 3, as said below
- live: int32 [16], replicated, may hold values from 1 to 512
Outputs:
- filtered: bfloat16 [2, 2048, 8192], P(None, 'ctx', 'ch')
The draws below stay inside these ranges and needn't reach their ends.
Inputs may be any that keep to these rules, and one draw needn't show every extreme that they name: `shard_doc`: documents occupy whole consecutive shards in order; each document spans 1 to 8 shards and one spans exactly 8. Read only for a shard that ends a document; its tokens at offsets from live on are padding.
All inputs are finite; a program needn't handle non-finite values.
Results may differ from the reference program's by a relative error of at most 0.012.
Values may be sent and summed in bfloat16 or wider, within the bound.
No kernel may reach another device: no remote copies, remote signals or barrier semaphores. Data moves between devices by JAX's collectives and lax.ppermute only.
A program may use at most 256 MiB of HBM per device.

```python
import jax
import jax.numpy as jnp

D = 4096
TOK_DEV = 512
FILT = 2048
SHARDS = 16
TOKENS = 8192
DOCS = 4
DOCMOST = 8
N_CH = 2


def draw_shard_doc(key, part):
    order_key = jax.random.fold_in(key, 11)
    place_key = jax.random.fold_in(key, 23)
    others = DOCS - 1
    rest = SHARDS - DOCMOST
    base_len = 1 + (rest - others) // others
    surplus = (rest - others) % others
    ranks = jax.random.permutation(order_key, others).astype(jnp.int32)
    small_lens = base_len + (ranks < surplus).astype(jnp.int32)
    where_big = jax.random.randint(place_key, (), 0, DOCS, dtype=jnp.int32)
    slots = jnp.arange(DOCS, dtype=jnp.int32)
    before = jnp.clip(slots, 0, others - 1)
    after = jnp.clip(slots - 1, 0, others - 1)
    all_lens = jnp.where(slots < where_big, small_lens[before], jnp.where(slots == where_big, DOCMOST, small_lens[after]))
    ends = jnp.cumsum(all_lens).astype(jnp.int32)
    shard_ids = jnp.arange(SHARDS, dtype=jnp.int32)
    return jnp.sum((shard_ids[:, None] >= ends[None, :]).astype(jnp.int32), axis=1).astype(jnp.int32)


def set_ends(result, own_key, low, high):
    index_at = [jax.random.randint(jax.random.fold_in(own_key, axis), (), 0, length) for axis, length in enumerate(result.shape)]
    widest = result.shape.index(max(result.shape))
    beside = index_at[:widest] + [(index_at[widest] + 1) % result.shape[widest]] + index_at[widest + 1:]
    return result.at[tuple(index_at)].set(low).at[tuple(beside)].set(high)


def steps_of(stream_key, extent, shards, low, largest):
    level, own = 1.0, jax.random.fold_in(stream_key, 6)
    for dim, parts in shards:
        draws = jnp.exp(jax.random.uniform(jax.random.fold_in(own, dim), (parts,), jnp.float32, low / len(shards), largest / len(shards)))
        level = level * jnp.repeat(draws, extent[dim] // parts).reshape([-1 if axis == dim else 1 for axis in range(len(extent))])
    return level


def bell_draw(key, shape, width, limit, pieces=(), kind=jnp.bfloat16):
    factor_of = steps_of(key, shape, pieces, -0.22, 0.18) if pieces else 1.0
    values = jax.random.normal(key, shape, jnp.float32) * width * factor_of
    return jnp.minimum(jnp.maximum(values, -limit), limit).astype(kind)


def setup_inputs(seed: int = 0) -> dict:
    key_list = jax.random.split(jax.random.key(seed), 7)
    qkv = bell_draw(key_list[0], (3, TOKENS, D), 1.0, 6.0, ((1, 16), (2, 2)))
    short_filter = bell_draw(key_list[1], (3, 3, D), 0.6, 3.0, ((2, 2),), jnp.float32)
    long_filter = bell_draw(key_list[2], (FILT, D), FILT ** -0.5, 0.125, ((1, 2),))
    skip = jnp.clip(jax.random.uniform(key_list[3], (D,), jnp.float32, -1.0, 1.0) * steps_of(key_list[3], (D,), ((0, 2),), -0.4, 0.0), -1.0, 1.0)
    shard_doc = draw_shard_doc(jax.random.fold_in(key_list[6], 71), 0)
    live = set_ends(jax.random.randint(key_list[5], (SHARDS,), 1, TOK_DEV + 1), jax.random.fold_in(key_list[5], 1), 1, TOK_DEV).astype(jnp.int32)
    return dict(qkv=qkv, short_filter=short_filter, long_filter=long_filter, skip=skip, shard_doc=shard_doc, live=live)


def reference(qkv, short_filter, long_filter, skip, shard_doc, live):
    tok_rows = TOK_DEV
    spans = FILT // TOK_DEV
    shard_total = SHARDS
    offsets = jnp.arange(tok_rows, dtype=jnp.int32)
    prev_doc = jnp.concatenate([jnp.full((1,), -1, jnp.int32), shard_doc[:-1]])
    next_doc = jnp.concatenate([shard_doc[1:], jnp.full((1,), -1, jnp.int32)])
    joined = prev_doc == shard_doc
    closing = next_doc != shard_doc
    keep = (jnp.logical_not(closing)[:, None] | (offsets[None, :] < live[:, None])).astype(jnp.float32).reshape(TOKENS, 1)
    link_one = ((offsets >= 1)[None, :] | joined[:, None]).astype(jnp.float32).reshape(TOKENS, 1)
    link_two = ((offsets >= 2)[None, :] | joined[:, None]).astype(jnp.float32).reshape(TOKENS, 1)

    def short_conv(index):
        signal = qkv[index].astype(jnp.float32)
        first = jnp.concatenate([jnp.zeros((1, D), jnp.float32), signal[:-1]], axis=0) * link_one
        second = jnp.concatenate([jnp.zeros((2, D), jnp.float32), signal[:-2]], axis=0) * link_two
        return short_filter[index, 0][None, :] * signal + short_filter[index, 1][None, :] * first + short_filter[index, 2][None, :] * second

    queries = short_conv(0).astype(jnp.bfloat16)
    gated = (short_conv(1) * short_conv(2) * keep).astype(jnp.bfloat16)
    blocks = gated.astype(jnp.float32).reshape(shard_total, tok_rows, D)
    spectra = jnp.fft.rfft(blocks, n=2 * tok_rows, axis=1)
    filter_spec = jnp.fft.rfft(long_filter.astype(jnp.float32).reshape(spans, tok_rows, D), n=2 * tok_rows, axis=1)
    totals = jnp.zeros_like(spectra)
    for lag_block in range(spans):
        source_doc = jnp.concatenate([jnp.full((lag_block,), -1, jnp.int32), shard_doc[:shard_total - lag_block]])
        shifted = jnp.concatenate([jnp.zeros((lag_block, tok_rows + 1, D), spectra.dtype), spectra[:shard_total - lag_block]], axis=0)
        totals = totals + jnp.where((source_doc == shard_doc)[:, None, None], filter_spec[lag_block][None] * shifted, 0)
    conv_full = jnp.fft.irfft(totals, n=2 * tok_rows, axis=1)
    spill = jnp.concatenate([jnp.zeros((1, tok_rows, D), conv_full.dtype), conv_full[:-1, tok_rows:]], axis=0)
    spill = spill * joined.astype(conv_full.dtype)[:, None, None]
    conv = (conv_full[:, :tok_rows] + spill).reshape(TOKENS, D)
    mixed = queries.astype(jnp.float32) * (conv + skip[None, :] * gated.astype(jnp.float32)) * keep
    return mixed.astype(jnp.bfloat16).T.reshape(N_CH, D // N_CH, TOKENS)
```

```python
import functools

import jax
import jax.numpy as jnp
from jax import lax
from jax.experimental import pallas as pl
from jax.experimental.pallas import tpu as pltpu
from jax.sharding import PartitionSpec as P

LANES = 128
UNROLL = 4
VMEM = 56 << 20


def short_kernel(doc, live, border, taps, qkv, qs_out, gated_out):
    shards = doc.shape[0]
    here = lax.axis_index("ctx")
    tok = qkv.shape[1]
    before = jnp.maximum(here - 1, 0)
    after = jnp.minimum(here + 1, shards - 1)
    joined = (here > 0) & (doc[before] == doc[here])
    closing = (here == shards - 1) | (doc[after] != doc[here])
    limit = jnp.where(closing, live[here], tok)

    def short(a):
        x = qkv[a].astype(jnp.float32)
        edge = jnp.where(joined, border[a].astype(jnp.float32), 0.0)
        once = jnp.concatenate([edge[1:2], x[:-1]], axis=0)
        twice = jnp.concatenate([edge, x[:-2]], axis=0)
        return taps[a, 0:1, :] * x + taps[a, 1:2, :] * once + taps[a, 2:3, :] * twice

    rows = lax.broadcasted_iota(jnp.int32, qkv.shape[1:], 0)
    keep = jnp.where(rows < limit, 1.0, 0.0)
    qs_out[...] = short(0).astype(jnp.bfloat16).T
    gated_out[...] = (short(1) * short(2) * keep).astype(jnp.bfloat16).T


def short_and_gate(qkv, border, short_filter, shard_doc, live):
    _, tok, width = qkv.shape
    block = min(256, width)
    smem = pl.BlockSpec(memory_space=pltpu.SMEM)
    out = pl.BlockSpec((block, tok), lambda i: (i, 0))
    return pl.pallas_call(
        short_kernel,
        grid=(width // block,),
        in_specs=[
            smem,
            smem,
            pl.BlockSpec((3, 2, block), lambda i: (0, 0, i)),
            pl.BlockSpec((3, 3, block), lambda i: (0, 0, i)),
            pl.BlockSpec((3, tok, block), lambda i: (0, 0, i)),
        ],
        out_specs=[out, out],
        out_shape=[jax.ShapeDtypeStruct((width, tok), jnp.bfloat16)] * 2,
        compiler_params=pltpu.CompilerParams(vmem_limit_bytes=VMEM),
        name="short_and_gate",
    )(shard_doc, live, border, short_filter, qkv)


def conv_kernel(doc, live, skip, filt, gated, queries, out, taps, masks, wide, one, mixed):
    shards, chans, tok = gated.shape
    per = tok // LANES
    blocks = shards * per
    lag_blocks = masks.shape[0]
    pad = lag_blocks - 1
    step = pl.program_id(0)

    @pl.when(step == 0)
    def _():
        taps[...] = filt[...].astype(jnp.float32).T
        wide[pl.ds(0, pad * chans), :] = jnp.zeros((pad * chans, LANES), jnp.float32)
        start = jnp.int32(0)
        rows = lax.broadcasted_iota(jnp.int32, (per, LANES), 0)
        runs = []
        for s in range(shards):
            if s > 0:
                start = jnp.where(doc[s] == doc[s - 1], start, s)
            runs.append(rows + (s - start) * per)
        run = jnp.concatenate(runs, axis=0)
        for k in range(lag_blocks):
            masks[k] = jnp.where(run >= k, 1.0, 0.0).astype(jnp.bfloat16)

    for s in range(shards):
        for b in range(per):
            rows = pl.ds((pad + s * per + b) * chans, chans)
            wide[rows, :] = gated[s, :, b * LANES : (b + 1) * LANES].astype(jnp.float32)

    def channel(c, slot):
        row = taps[pl.ds(step * chans + c, 1), :]
        row = jnp.concatenate([row, jnp.zeros((1, LANES), jnp.float32)], axis=1)
        spread = jnp.broadcast_to(row, (16, row.shape[1]))
        band = pltpu.roll(spread, 0, 1, stride=1, stride_axis=0).astype(jnp.bfloat16)
        bands = [band] + [pltpu.roll(band, 16 * q, 1) for q in range(1, LANES // 16)]
        toeplitz = jnp.concatenate(bands, axis=0)
        weights = jnp.concatenate(
            [toeplitz[:, k * LANES : (k + 1) * LANES] for k in range(lag_blocks)], axis=0
        )
        one[slot] = wide[pl.ds(c, blocks + pad, stride=chans), :]
        lagged = [
            one[slot, pl.ds(pad - k, blocks), :].astype(jnp.bfloat16) * masks[k]
            for k in range(lag_blocks)
        ]
        mixed[pl.ds(c, blocks, stride=chans), :] = jnp.dot(
            jnp.concatenate(lagged, axis=1), weights, preferred_element_type=jnp.float32
        )

    def group(i, _):
        for slot in range(UNROLL):
            channel(i * UNROLL + slot, slot)
        return 0

    lax.fori_loop(0, chans // UNROLL, group, 0)

    direct = skip[...]
    places = lax.broadcasted_iota(jnp.int32, (1, tok), 1)
    for s in range(shards):
        if s < shards - 1:
            limit = jnp.where(doc[s] != doc[s + 1], live[s], tok)
        else:
            limit = live[s]
        keep = jnp.where(places < limit, 1.0, 0.0)
        conv = jnp.concatenate(
            [mixed[pl.ds((s * per + b) * chans, chans), :] for b in range(per)], axis=1
        )
        total = conv + direct * gated[s].astype(jnp.float32)
        done = queries[s].astype(jnp.float32) * total * keep
        halves, _, half_tok = out.shape
        first = s * tok
        out[first // half_tok, :, pl.ds(first % half_tok, tok)] = done.astype(jnp.bfloat16)


def long_conv(gated, queries, filt, skip, shard_doc, live, halves):
    shards, width, tok = gated.shape
    lags = filt.shape[0]
    chans = min(32, width)
    blocks = shards * tok // LANES
    lag_blocks = lags // LANES + 1
    half_tok = shards * tok // halves
    smem = pl.BlockSpec(memory_space=pltpu.SMEM)
    slab = pl.BlockSpec((shards, chans, tok), lambda i: (0, i, 0))
    return pl.pallas_call(
        conv_kernel,
        grid=(width // chans,),
        in_specs=[
            smem,
            smem,
            pl.BlockSpec((chans, 1), lambda i: (i, 0)),
            pl.BlockSpec((lags, width), lambda i: (0, 0)),
            slab,
            slab,
        ],
        out_specs=pl.BlockSpec((halves, chans, half_tok), lambda i: (0, i, 0)),
        out_shape=jax.ShapeDtypeStruct((halves, width, half_tok), jnp.bfloat16),
        scratch_shapes=[
            pltpu.VMEM((width, lags), jnp.float32),
            pltpu.VMEM((lag_blocks, blocks, LANES), jnp.bfloat16),
            pltpu.VMEM(((blocks + lag_blocks - 1) * chans, LANES), jnp.float32),
            pltpu.VMEM((UNROLL, blocks + lag_blocks - 1, LANES), jnp.float32),
            pltpu.VMEM((blocks * chans, LANES), jnp.float32),
        ],
        compiler_params=pltpu.CompilerParams(
            vmem_limit_bytes=VMEM, dimension_semantics=("arbitrary",)
        ),
        name="long_conv",
    )(shard_doc, live, skip[:, None], filt, gated, queries)


def local(qkv, short_filter, long_filter, skip, shard_doc, live):
    shards = lax.axis_size("ctx")
    here = lax.axis_index("ctx")
    tok, width = qkv.shape[1:]
    part = width // shards
    route = [(i, i + 1) for i in range(shards - 1)]
    border = lax.ppermute(qkv[:, tok - 2 :, :], "ctx", route)
    queries, gated = short_and_gate(qkv, border, short_filter, shard_doc, live)
    gated = lax.all_to_all(gated.reshape(shards, part, tok), "ctx", 0, 0)
    queries = lax.all_to_all(queries.reshape(shards, part, tok), "ctx", 0, 0)
    filt = lax.dynamic_slice_in_dim(long_filter, here * part, part, axis=1)
    direct = lax.dynamic_slice_in_dim(skip, here * part, part, axis=0)
    out = long_conv(gated, queries, filt, direct, shard_doc, live, lax.axis_size("ch"))
    return lax.all_to_all(out, "ch", 0, 0)


def solution(mesh):
    return jax.shard_map(
        local,
        mesh=mesh,
        in_specs=(P(None, "ctx", "ch"), P(None, None, "ch"), P(None, "ch"), P("ch"), P(), P()),
        out_specs=P(None, "ctx", "ch"),
        check_vma=False,
    )
```

```python
import functools

import jax
import jax.numpy as jnp
from jax import lax
from jax.experimental import pallas as pl
from jax.experimental.pallas import tpu as pltpu
from jax.sharding import PartitionSpec as P

LANES = 128
UNROLL = 8
ROWS = 64
CORES = 2
FLYING = 5
VMEM = 56 << 20


def short_kernel(count, doc, live, *refs):
    borders, taps, slabs = refs[:count], refs[count : 2 * count], refs[2 * count : 3 * count]
    outs, tall, turned = refs[3 * count : -2], refs[-2], refs[-1]
    shards = doc.shape[0]
    here = lax.axis_index("ctx")
    tok = slabs[0].shape[1]
    before = jnp.maximum(here - 1, 0)
    after = jnp.minimum(here + 1, shards - 1)
    joined = (here > 0) & (doc[before] == doc[here])
    closing = (here == shards - 1) | (doc[after] != doc[here])
    limit = jnp.where(closing, live[here], tok)

    def short(a):
        x = slabs[a][0].astype(jnp.float32)
        edge = jnp.where(joined, borders[a][0].astype(jnp.float32), 0.0)
        tall[a, 6:8, :] = edge
        tall[a, pl.ds(8, tok), :] = x
        once = tall[a, pl.ds(7, tok), :]
        twice = tall[a, pl.ds(6, tok), :]
        tap = taps[a]
        return tap[0, 0:1, :] * x + tap[0, 1:2, :] * once + tap[0, 2:3, :] * twice

    value = short(0)
    if count == 2:
        rows = lax.broadcasted_iota(jnp.int32, value.shape, 0)
        value = value * short(1) * jnp.where(rows < limit, 1.0, 0.0)
    value = value.astype(jnp.bfloat16).T
    if len(outs) == 1:
        part = outs[0].shape[1]
        for j in range(outs[0].shape[0]):
            outs[0][j] = value[j * part : (j + 1) * part]
    else:
        turned[...] = value
        part = outs[0].shape[1]
        for k, out in enumerate(outs):
            for j in range(out.shape[0]):
                row = (CORES * j + ((here % CORES) ^ k)) * part
                out[j] = turned[pl.ds(pl.multiple_of(row, part), part), :]


def short_convs(qkv, border, short_filter, shard_doc, live, which, split):
    _, tok, width = qkv.shape
    shards = shard_doc.shape[0]
    part = width // shards
    block = min(width, 512)
    smem = pl.BlockSpec(memory_space=pltpu.SMEM)
    count = len(which)

    def spec(rows, a):
        return pl.BlockSpec((1, rows, block), lambda i: (a, 0, i))

    many = CORES if split else 1
    rows = block // part // many
    return pl.pallas_call(
        functools.partial(short_kernel, count),
        grid=(width // block,),
        in_specs=[smem] * 2
        + [spec(2, a) for a in which]
        + [spec(3, a) for a in which]
        + [spec(tok, a) for a in which],
        out_specs=[pl.BlockSpec((rows, part, tok), lambda i: (i, 0, 0))] * many,
        out_shape=[jax.ShapeDtypeStruct((shards // many, part, tok), jnp.bfloat16)] * many,
        scratch_shapes=[
            pltpu.VMEM((count, tok + 8, block), jnp.float32),
            pltpu.VMEM((block, tok), jnp.bfloat16),
        ],
        compiler_params=pltpu.CompilerParams(vmem_limit_bytes=VMEM),
        name="short_" + "".join("qkv"[a] for a in which),
    )(shard_doc, live, *[border] * count, *[short_filter] * count, *[qkv] * count)


def pair_up_kernel(*refs):
    blocks, outs = refs[:CORES], refs[CORES:]
    here = lax.axis_index("ctx")
    for k, block in enumerate(blocks):
        row = (here % CORES) ^ k
        for far, out in enumerate(outs):
            out[row] = block[(here // CORES) ^ far]


def pair_up(blocks):
    chips, part, tok = blocks[0].shape
    vmem = pl.BlockSpec(memory_space=pltpu.VMEM)
    return pl.pallas_call(
        pair_up_kernel,
        in_specs=[vmem] * CORES,
        out_specs=[vmem] * chips,
        out_shape=[jax.ShapeDtypeStruct((CORES, part, tok), jnp.bfloat16)] * chips,
        compiler_params=pltpu.CompilerParams(vmem_limit_bytes=VMEM),
        name="pair_up",
    )(*blocks)


def conv_kernel(doc, live, skip, filt, gated, out, taps, masks, wide, one, late, mixed):
    shards, chans, tok = gated.shape
    pitch = chans + 1
    per = tok // LANES
    fine = tok // ROWS
    blocks = shards * fine
    pairs = masks.shape[0] - 1
    pad = 8 * (pairs - 1)
    step = pl.program_id(0)
    lags = taps.shape[1]
    spans = lags // (4 * ROWS) + 1

    @pl.when(step == 0)
    def _():
        taps[...] = filt[...].astype(jnp.float32).T
        wide[pl.ds(0, pad * pitch), :] = jnp.zeros((pad * pitch, LANES), jnp.float32)
        late[:, pl.ds(0, 8), :] = jnp.zeros((late.shape[0], 8, LANES), jnp.float32)
        start = jnp.int32(0)
        rows = lax.broadcasted_iota(jnp.int32, (fine, LANES), 0)
        left = lax.broadcasted_iota(jnp.int32, (blocks, LANES), 1) < ROWS
        runs = []
        for s in range(shards):
            if s > 0:
                start = jnp.where(doc[s] == doc[s - 1], start, s)
            runs.append(rows + (s - start) * fine)
        run = jnp.concatenate(runs, axis=0)
        for m in range(pairs):
            reach = jnp.where(left, 8 * m, 8 * m + 4)
            masks[m] = jnp.where(run >= reach, 1.0, 0.0).astype(jnp.bfloat16)
        masks[pairs] = jnp.where(run >= 2, 1.0, 0.0).astype(jnp.bfloat16)

    left = lax.broadcasted_iota(jnp.int32, (chans, LANES), 1) < ROWS
    older = [(jnp.zeros((chans, LANES), jnp.float32),) * 2] * 2
    for s in range(shards):
        for b in range(per):
            here = gated[s, :, b * LANES : (b + 1) * LANES].astype(jnp.float32)
            turned = pltpu.roll(here, ROWS, 1)
            row = pad + s * fine + 2 * b
            wide[pl.ds(row * pitch, chans), :] = jnp.where(left, here, older[0][1])
            wide[pl.ds((row + 1) * pitch, chans), :] = jnp.where(left, turned, older[0][0])
            older = [older[1], (here, turned)]

    def channel(c, slot):
        row = taps[pl.ds(step * chans + c, 1), :]
        row = jnp.concatenate([row, jnp.zeros((1, 4 * ROWS), jnp.float32)], axis=1)
        spread = jnp.broadcast_to(row, (16, row.shape[1]))
        band = pltpu.roll(spread, 0, 1, stride=1, stride_axis=0).astype(jnp.bfloat16)
        bands = [band] + [pltpu.roll(band, 16 * q, 1) for q in range(1, ROWS // 16)]
        toeplitz = jnp.concatenate(bands, axis=0)
        slices = [toeplitz[:, k * 4 * ROWS : (k + 1) * 4 * ROWS] for k in range(spans)]
        slices += [jnp.zeros_like(slices[0])] * (2 * pairs - spans)
        weights = jnp.concatenate(slices, axis=0)
        one[slot] = wide[pl.ds(c, blocks + pad, stride=pitch), :]
        lagged = [
            one[slot, pl.ds(pad - 8 * m, blocks), :].astype(jnp.bfloat16) * masks[m]
            for m in range(pairs)
        ]
        sums = jnp.dot(
            jnp.concatenate(lagged, axis=1), weights, preferred_element_type=jnp.float32
        )
        late[slot, pl.ds(8, blocks), :] = sums[:, LANES:]
        behind = late[slot, pl.ds(6, blocks), :] * masks[pairs].astype(jnp.float32)
        mixed[pl.ds(c, blocks, stride=pitch), :] = sums[:, :LANES] + behind

    def group(i, _):
        for slot in range(UNROLL):
            channel(i * UNROLL + slot, slot)
        return 0

    lax.fori_loop(0, chans // UNROLL, group, 0)

    direct = skip[...]
    places = lax.broadcasted_iota(jnp.int32, (1, tok), 1)
    for s in range(shards):
        if s < shards - 1:
            limit = jnp.where(doc[s] != doc[s + 1], live[s], tok)
        else:
            limit = live[s]
        keep = jnp.where(places < limit, 1.0, 0.0)
        sums = []
        for b in range(per):
            row = s * fine + 2 * b
            after = mixed[pl.ds((row + 1) * pitch, chans), :]
            if row > 0:
                spill = mixed[pl.ds((row - 1) * pitch, chans), :]
                if b == 0:
                    spill = jnp.where(doc[s] == doc[s - 1], spill, 0.0)
            else:
                spill = jnp.zeros_like(after)
            sums.append(
                mixed[pl.ds(row * pitch, chans), :]
                + pltpu.roll(jnp.where(left, after, spill), ROWS, 1)
            )
        conv = jnp.concatenate(sums, axis=1)
        total = (conv + direct * gated[s].astype(jnp.float32)) * keep
        out[s] = total.astype(jnp.bfloat16)


def long_conv(gated, filt, skip, shard_doc, live):
    shards, width, tok = gated.shape
    lags, part = filt.shape
    chans = min(32, width)
    blocks = shards * tok // ROWS
    pairs = (lags // (4 * ROWS) + 2) // 2
    tall = blocks + 8 * (pairs - 1)
    smem = pl.BlockSpec(memory_space=pltpu.SMEM)
    slab = pl.BlockSpec((shards, chans, tok), lambda i: (0, i, 0))
    return pl.pallas_call(
        conv_kernel,
        grid=(width // chans,),
        in_specs=[
            smem,
            smem,
            pl.BlockSpec((chans, 1), lambda i: (i, 0)),
            pl.BlockSpec((lags, part), lambda i: (0, 0)),
            slab,
        ],
        out_specs=slab,
        out_shape=jax.ShapeDtypeStruct((shards, width, tok), jnp.bfloat16),
        scratch_shapes=[
            pltpu.VMEM((part, lags), jnp.float32),
            pltpu.VMEM((pairs + 1, blocks, LANES), jnp.bfloat16),
            pltpu.VMEM((tall * (chans + 1), LANES), jnp.float32),
            pltpu.VMEM((UNROLL, tall, LANES), jnp.float32),
            pltpu.VMEM((UNROLL, blocks + 8, LANES), jnp.float32),
            pltpu.VMEM((blocks * (chans + 1), LANES), jnp.float32),
        ],
        compiler_params=pltpu.CompilerParams(
            vmem_limit_bytes=VMEM, dimension_semantics=("arbitrary",)
        ),
        cost_estimate=pl.CostEstimate(
            flops=2 * width * shards * tok * lags,
            bytes_accessed=width * shards * tok * 4 + lags * part * 2,
            transcendentals=0,
        ),
        name="long_conv",
    )(shard_doc, live, skip, filt, gated)


def gate_kernel(fars, *refs):
    blocks, conv, own, sent = refs[:-3], refs[-3], refs[-2], refs[-1]
    shards, _, tok = conv.shape
    halves = sent.shape[0] + 1
    per = shards // halves
    span = len(fars) // halves
    here = lax.axis_index("ctx")
    mine = lax.axis_index("ch")
    for far, block in zip(fars, blocks):
        chip = (here // CORES) ^ far
        first = chip * CORES
        away = (first // per + halves - mine) % halves
        values = [
            (block[k].astype(jnp.float32) * conv[first + k].astype(jnp.float32)).astype(
                jnp.bfloat16
            )
            for k in range(CORES)
        ]
        value = jnp.concatenate(values, axis=1)
        start = chip % span * (CORES * tok)
        column = pl.ds(pl.multiple_of(start, CORES * tok), CORES * tok)

        @pl.when(away == 0)
        def _():
            own[:, column] = value

        @pl.when(away != 0)
        def _():
            sent[away - 1, :, column] = value


def gate(fars, blocks, conv, halves):
    _, width, tok = blocks[0].shape
    shards = conv.shape[0]
    chans = min(64, width)
    wide = len(fars) // halves * CORES * tok
    return pl.pallas_call(
        functools.partial(gate_kernel, fars),
        grid=(width // chans,),
        in_specs=[pl.BlockSpec((CORES, chans, tok), lambda i: (0, i, 0))] * len(blocks)
        + [pl.BlockSpec((shards, chans, tok), lambda i: (0, i, 0))],
        out_specs=[
            pl.BlockSpec((chans, wide), lambda i: (i, 0)),
            pl.BlockSpec((halves - 1, chans, wide), lambda i: (0, i, 0)),
        ],
        out_shape=[
            jax.ShapeDtypeStruct((width, wide), jnp.bfloat16),
            jax.ShapeDtypeStruct((halves - 1, width, wide), jnp.bfloat16),
        ],
        compiler_params=pltpu.CompilerParams(vmem_limit_bytes=VMEM),
        name="gate",
    )(*blocks, conv)


def local(qkv, short_filter, long_filter, skip, shard_doc, live):
    shards = lax.axis_size("ctx")
    halves = lax.axis_size("ch")
    here = lax.axis_index("ctx")
    mine = lax.axis_index("ch")
    tok, width = qkv.shape[1:]
    part = width // shards
    chips = shards // CORES
    span = chips // halves
    border = lax.ppermute(
        qkv[:, tok - 2 :, :], "ctx", [(i, i + 1) for i in range(shards - 1)]
    )
    filt = lax.dynamic_slice_in_dim(long_filter, here * part, part, axis=1)
    direct = lax.dynamic_slice_in_dim(skip, here * part, part, axis=0)[:, None]
    out = jnp.zeros((halves, part, shards * tok // halves), jnp.bfloat16)

    def short(which, split):
        return short_convs(qkv, border, short_filter, shard_doc, live, which, split)

    def across(block, distance):
        return lax.ppermute(block, "ctx", [(i, i ^ distance) for i in range(shards)])

    (gated,) = short((1, 2), False)
    qkv, gated = lax.optimization_barrier((qkv, gated))
    queries = short((0,), True)
    gated = lax.all_to_all(gated, "ctx", 0, 0)
    queries = [queries[0]] + [across(queries[k], k) for k in range(1, CORES)]
    queries = pair_up(queries)
    cuts = [0, span // 2, span * 3 // 4, span]
    groups = [
        [near + h * span for near in range(low, high) for h in reversed(range(halves))]
        for low, high in zip(cuts, cuts[1:])
    ]
    order = [far for fars in groups for far in fars if far]
    got = {0: queries[0]}

    def launch(fars, after):
        blocks, after = lax.optimization_barrier(([queries[far] for far in fars], after))
        for far, block in zip(fars, blocks):
            got[far] = across(block, far * CORES)
        return after

    gated = launch(order[:FLYING], gated)
    conv = long_conv(gated, filt, direct, shard_doc, live)
    conv = launch(order[FLYING:], conv)
    arrived = [[got[far] for far in fars] for fars in groups]
    for fars, blocks in zip(groups, arrived):
        own, sent = gate(fars, blocks, conv, halves)
        wide = own.shape[1]
        first = (here // CORES) % span ^ fars[-1]
        start = first // (len(fars) // halves) * wide
        out = lax.dynamic_update_slice(out, own[None], (mine, 0, start))
        for d in range(1, halves):
            route = [(j, (j + d) % halves) for j in range(halves)]
            came = lax.ppermute(sent[d - 1], "ch", route)
            source = lax.rem(mine + halves - d, halves)
            out = lax.dynamic_update_slice(out, came[None], (source, 0, start))
    return out


def solution(mesh):
    return jax.shard_map(
        local,
        mesh=mesh,
        in_specs=(P(None, "ctx", "ch"), P(None, None, "ch"), P(None, "ch"), P("ch"), P(), P()),
        out_specs=P(None, "ctx", "ch"),
        check_vma=False,
    )
```

```python
import functools

import jax
import jax.numpy as jnp
from jax import lax
from jax.experimental import pallas as pl
from jax.experimental.pallas import tpu as pltpu
from jax.sharding import PartitionSpec as P

LANES = 128
UNROLL = 8
ROWS = 64
CORES = 2
FLYING = 6
CHANS = 32
VMEM = 56 << 20


def shard_facts(doc, live, tok):
    shards = doc.shape[0]
    here = lax.axis_index("ctx")
    before = jnp.maximum(here - 1, 0)
    after = jnp.minimum(here + 1, shards - 1)
    joined = (here > 0) & (doc[before] == doc[here])
    closing = (here == shards - 1) | (doc[after] != doc[here])
    return joined, jnp.where(closing, live[here], tok)


def short_kernel(count, edges, doc, live, *refs):
    taps, slabs = refs[:count], refs[count : 2 * count]
    borders, refs = refs[2 * count : 2 * count + edges], refs[2 * count + edges :]
    outs, tall, turned = refs[:-2], refs[-2], refs[-1]
    here = lax.axis_index("ctx")
    tok = slabs[0].shape[1]
    joined, limit = shard_facts(doc, live, tok)

    def short(a):
        x = slabs[a][0].astype(jnp.float32)
        edge = jnp.zeros((2, x.shape[1]), jnp.float32)
        if edges:
            edge = jnp.where(joined, borders[a][0].astype(jnp.float32), 0.0)
        tall[a, 6:8, :] = edge
        tall[a, pl.ds(8, tok), :] = x
        once = tall[a, pl.ds(7, tok), :]
        twice = tall[a, pl.ds(6, tok), :]
        tap = taps[a]
        return tap[0, 0:1, :] * x + tap[0, 1:2, :] * once + tap[0, 2:3, :] * twice

    value = short(0)
    if count == 2:
        rows = lax.broadcasted_iota(jnp.int32, value.shape, 0)
        value = value * short(1) * jnp.where(rows < limit, 1.0, 0.0)
    value = value.astype(jnp.bfloat16).T
    if len(outs) == 1:
        part = outs[0].shape[1]
        for j in range(outs[0].shape[0]):
            outs[0][j] = value[j * part : (j + 1) * part]
    else:
        turned[...] = value
        part = outs[0].shape[1]
        for k, out in enumerate(outs):
            for j in range(out.shape[0]):
                row = (CORES * j + ((here % CORES) ^ k)) * part
                out[j] = turned[pl.ds(pl.multiple_of(row, part), part), :]


def short_convs(qkv, short_filter, shard_doc, live, which, split, border=None):
    _, tok, width = qkv.shape
    shards = shard_doc.shape[0]
    part = width // shards
    block = min(width, 512)
    smem = pl.BlockSpec(memory_space=pltpu.SMEM)
    count = len(which)
    borders = [] if border is None else [border] * count

    def spec(rows, a):
        return pl.BlockSpec((1, rows, block), lambda i: (a, 0, i))

    many = CORES if split else 1
    rows = block // part // many
    return pl.pallas_call(
        functools.partial(short_kernel, count, len(borders)),
        grid=(width // block,),
        in_specs=[smem] * 2
        + [spec(3, a) for a in which]
        + [spec(tok, a) for a in which]
        + [spec(2, a) for a in which if border is not None],
        out_specs=[pl.BlockSpec((rows, part, tok), lambda i: (i, 0, 0))] * many,
        out_shape=[jax.ShapeDtypeStruct((shards // many, part, tok), jnp.bfloat16)] * many,
        scratch_shapes=[
            pltpu.VMEM((count, tok + 8, block), jnp.float32),
            pltpu.VMEM((block, tok), jnp.bfloat16),
        ],
        compiler_params=pltpu.CompilerParams(vmem_limit_bytes=VMEM),
        name="short_" + "".join("qkv"[a] for a in which),
    )(shard_doc, live, *[short_filter] * count, *[qkv] * count, *borders)


def first_kernel(doc, live, key_edge, value_edge, key_taps, value_taps, key, value, old, out):
    shards, part, _ = old.shape
    tok = 2
    joined, limit = shard_facts(doc, live, tok)

    def short(edge, taps, slab):
        x = slab[0, :tok, :].astype(jnp.float32)
        edge = jnp.where(joined, edge[0].astype(jnp.float32), 0.0)
        once = jnp.concatenate([edge[1:], x[:1]], axis=0)
        return taps[0, 0:1, :] * x + taps[0, 1:2, :] * once + taps[0, 2:3, :] * edge

    keep = jnp.where(lax.broadcasted_iota(jnp.int32, (tok, 1), 0) < limit, 1.0, 0.0)
    both = short(key_edge, key_taps, key) * short(value_edge, value_taps, value) * keep
    tall = jnp.concatenate([both, jnp.zeros((LANES - tok, both.shape[1]), jnp.float32)], axis=0)
    new = tall.astype(jnp.bfloat16).T.reshape(shards, part, LANES)
    place = lax.broadcasted_iota(jnp.int32, new.shape, 2)
    out[...] = jnp.where(place < tok, new, old[...])


def first_tokens(gated, qkv, border, short_filter, shard_doc, live):
    shards, part, _ = gated.shape
    width = shards * part
    smem = pl.BlockSpec(memory_space=pltpu.SMEM)

    def spec(rows, a):
        return pl.BlockSpec((1, rows, width), lambda i: (a, 0, 0))

    tile = pl.BlockSpec((shards, part, LANES), lambda i: (0, 0, 0))
    return pl.pallas_call(
        first_kernel,
        grid=(1,),
        in_specs=[smem] * 2 + [spec(rows, a) for rows in (2, 3, 16) for a in (1, 2)] + [tile],
        out_specs=tile,
        out_shape=jax.ShapeDtypeStruct(gated.shape, gated.dtype),
        input_output_aliases={8: 0},
        compiler_params=pltpu.CompilerParams(vmem_limit_bytes=VMEM),
        name="first_tokens",
    )(shard_doc, live, *[border] * 2, *[short_filter] * 2, *[qkv] * 2, gated)


def pair_up_kernel(*refs):
    blocks, outs = refs[:CORES], refs[CORES:]
    here = lax.axis_index("ctx")
    for k, block in enumerate(blocks):
        row = (here % CORES) ^ k
        for far, out in enumerate(outs):
            out[row] = block[(here // CORES) ^ far]


def pair_up(blocks):
    chips, part, tok = blocks[0].shape
    vmem = pl.BlockSpec(memory_space=pltpu.VMEM)
    return pl.pallas_call(
        pair_up_kernel,
        in_specs=[vmem] * CORES,
        out_specs=[vmem] * chips,
        out_shape=[jax.ShapeDtypeStruct((CORES, part, tok), jnp.bfloat16)] * chips,
        compiler_params=pltpu.CompilerParams(vmem_limit_bytes=VMEM),
        name="pair_up",
    )(*blocks)


def prepare_kernel(filt, out, taps):
    step = pl.program_id(0)
    chans, rows, width = out.shape

    @pl.when(step == 0)
    def _():
        taps[...] = filt[...].astype(jnp.float32).T

    def channel(c, _):
        row = taps[pl.ds(step * chans + c, 1), :]
        row = jnp.concatenate([row, jnp.zeros((1, width), jnp.float32)], axis=1)
        spread = jnp.broadcast_to(row, (16, row.shape[1]))
        band = pltpu.roll(spread, 0, 1, stride=1, stride_axis=0).astype(jnp.bfloat16)
        bands = [band] + [pltpu.roll(band, 16 * q, 1) for q in range(1, ROWS // 16)]
        toeplitz = jnp.concatenate(bands, axis=0)
        for k in range(rows // ROWS):
            out[c, k * ROWS : (k + 1) * ROWS, :] = toeplitz[:, k * width : (k + 1) * width]
        return 0

    lax.fori_loop(0, chans, channel, 0, unroll=4)


def prepare(filt):
    lags, part = filt.shape
    chans = min(CHANS, part)
    width = 4 * ROWS
    rows = (lags // width + 1) * ROWS
    return pl.pallas_call(
        prepare_kernel,
        grid=(part // chans,),
        in_specs=[pl.BlockSpec((lags, part), lambda i: (0, 0))],
        out_specs=pl.BlockSpec((chans, rows, width), lambda i: (i, 0, 0)),
        out_shape=jax.ShapeDtypeStruct((part, rows, width), jnp.bfloat16),
        scratch_shapes=[pltpu.VMEM((part, lags), jnp.float32)],
        compiler_params=pltpu.CompilerParams(
            vmem_limit_bytes=VMEM, dimension_semantics=("arbitrary",)
        ),
        name="prepare",
    )(filt)


def conv_kernel(doc, live, skip, toeplitz, gated, out, masks, wide, one, late, mixed):
    shards, chans, tok = gated.shape
    pitch = chans + 1
    per = tok // LANES
    fine = tok // ROWS
    blocks = shards * fine
    pairs = masks.shape[0] - 1
    pad = 8 * (pairs - 1)
    step = pl.program_id(0)
    depth = toeplitz.shape[1]

    @pl.when(step == 0)
    def _():
        wide[pl.ds(0, pad * pitch), :] = jnp.zeros((pad * pitch, LANES), jnp.float32)
        late[:, pl.ds(0, 8), :] = jnp.zeros((late.shape[0], 8, LANES), jnp.float32)
        start = jnp.int32(0)
        rows = lax.broadcasted_iota(jnp.int32, (fine, LANES), 0)
        left = lax.broadcasted_iota(jnp.int32, (blocks, LANES), 1) < ROWS
        runs = []
        for s in range(shards):
            if s > 0:
                start = jnp.where(doc[s] == doc[s - 1], start, s)
            runs.append(rows + (s - start) * fine)
        run = jnp.concatenate(runs, axis=0)
        for m in range(pairs):
            reach = jnp.where(left, 8 * m, 8 * m + 4)
            masks[m] = jnp.where(run >= reach, 1.0, 0.0).astype(jnp.bfloat16)
        masks[pairs] = jnp.where(run >= 2, 1.0, 0.0).astype(jnp.bfloat16)

    left = lax.broadcasted_iota(jnp.int32, (chans, LANES), 1) < ROWS
    older = [(jnp.zeros((chans, LANES), jnp.float32),) * 2] * 2
    for s in range(shards):
        for b in range(per):
            here = gated[s, :, b * LANES : (b + 1) * LANES].astype(jnp.float32)
            turned = pltpu.roll(here, ROWS, 1)
            row = pad + s * fine + 2 * b
            wide[pl.ds(row * pitch, chans), :] = jnp.where(left, here, older[0][1])
            wide[pl.ds((row + 1) * pitch, chans), :] = jnp.where(left, turned, older[0][0])
            older = [older[1], (here, turned)]

    def channel(c, slot):
        one[slot] = wide[pl.ds(c, blocks + pad, stride=pitch), :]
        lagged = [
            one[slot, pl.ds(pad - 8 * m, blocks), :].astype(jnp.bfloat16) * masks[m]
            for m in range(pairs)
        ]
        sums = jnp.dot(
            jnp.concatenate(lagged, axis=1)[:, :depth],
            toeplitz[c],
            preferred_element_type=jnp.float32,
        )
        late[slot, pl.ds(8, blocks), :] = sums[:, LANES:]
        behind = late[slot, pl.ds(6, blocks), :] * masks[pairs].astype(jnp.float32)
        mixed[pl.ds(c, blocks, stride=pitch), :] = sums[:, :LANES] + behind

    def group(i, _):
        for slot in range(UNROLL):
            channel(i * UNROLL + slot, slot)
        return 0

    lax.fori_loop(0, chans // UNROLL, group, 0)

    direct = skip[...]
    places = lax.broadcasted_iota(jnp.int32, (1, tok), 1)
    for s in range(shards):
        if s < shards - 1:
            limit = jnp.where(doc[s] != doc[s + 1], live[s], tok)
        else:
            limit = live[s]
        keep = jnp.where(places < limit, 1.0, 0.0)
        sums = []
        for b in range(per):
            row = s * fine + 2 * b
            after = mixed[pl.ds((row + 1) * pitch, chans), :]
            if row > 0:
                spill = mixed[pl.ds((row - 1) * pitch, chans), :]
                if b == 0:
                    spill = jnp.where(doc[s] == doc[s - 1], spill, 0.0)
            else:
                spill = jnp.zeros_like(after)
            sums.append(
                mixed[pl.ds(row * pitch, chans), :]
                + pltpu.roll(jnp.where(left, after, spill), ROWS, 1)
            )
        conv = jnp.concatenate(sums, axis=1)
        total = (conv + direct * gated[s].astype(jnp.float32)) * keep
        out[s] = total.astype(jnp.bfloat16)


def long_conv(gated, toeplitz, skip, shard_doc, live):
    shards, width, tok = gated.shape
    depth = toeplitz.shape[1]
    chans = min(CHANS, width)
    blocks = shards * tok // ROWS
    pairs = (depth // ROWS + 1) // 2
    tall = blocks + 8 * (pairs - 1)
    smem = pl.BlockSpec(memory_space=pltpu.SMEM)
    slab = pl.BlockSpec((shards, chans, tok), lambda i: (0, i, 0))
    return pl.pallas_call(
        conv_kernel,
        grid=(width // chans,),
        in_specs=[
            smem,
            smem,
            pl.BlockSpec((chans, 1), lambda i: (i, 0)),
            pl.BlockSpec((chans, depth, 4 * ROWS), lambda i: (i, 0, 0)),
            slab,
        ],
        out_specs=slab,
        out_shape=jax.ShapeDtypeStruct((shards, width, tok), jnp.bfloat16),
        scratch_shapes=[
            pltpu.VMEM((pairs + 1, blocks, LANES), jnp.bfloat16),
            pltpu.VMEM((tall * (chans + 1), LANES), jnp.float32),
            pltpu.VMEM((UNROLL, tall, LANES), jnp.float32),
            pltpu.VMEM((UNROLL, blocks + 8, LANES), jnp.float32),
            pltpu.VMEM((blocks * (chans + 1), LANES), jnp.float32),
        ],
        compiler_params=pltpu.CompilerParams(
            vmem_limit_bytes=VMEM, dimension_semantics=("arbitrary",)
        ),
        cost_estimate=pl.CostEstimate(flops=1, bytes_accessed=1, transcendentals=0),
        name="long_conv",
    )(shard_doc, live, skip, toeplitz, gated)


def gate_kernel(fars, *refs):
    blocks, conv, own, sent = refs[:-3], refs[-3], refs[-2], refs[-1]
    shards, _, tok = conv.shape
    halves = sent.shape[0] + 1
    per = shards // halves
    span = len(fars) // halves
    here = lax.axis_index("ctx")
    mine = lax.axis_index("ch")
    for far, block in zip(fars, blocks):
        chip = (here // CORES) ^ far
        first = chip * CORES
        away = (first // per + halves - mine) % halves
        values = [
            (block[k].astype(jnp.float32) * conv[first + k].astype(jnp.float32)).astype(
                jnp.bfloat16
            )
            for k in range(CORES)
        ]
        value = jnp.concatenate(values, axis=1)
        start = chip % span * (CORES * tok)
        column = pl.ds(pl.multiple_of(start, CORES * tok), CORES * tok)

        @pl.when(away == 0)
        def _():
            own[:, column] = value

        @pl.when(away != 0)
        def _():
            sent[away - 1, :, column] = value


def gate(fars, blocks, conv, halves):
    _, width, tok = blocks[0].shape
    shards = conv.shape[0]
    chans = min(64, width)
    wide = len(fars) // halves * CORES * tok
    return pl.pallas_call(
        functools.partial(gate_kernel, fars),
        grid=(width // chans,),
        in_specs=[pl.BlockSpec((CORES, chans, tok), lambda i: (0, i, 0))] * len(blocks)
        + [pl.BlockSpec((shards, chans, tok), lambda i: (0, i, 0))],
        out_specs=[
            pl.BlockSpec((chans, wide), lambda i: (i, 0)),
            pl.BlockSpec((halves - 1, chans, wide), lambda i: (0, i, 0)),
        ],
        out_shape=[
            jax.ShapeDtypeStruct((width, wide), jnp.bfloat16),
            jax.ShapeDtypeStruct((halves - 1, width, wide), jnp.bfloat16),
        ],
        compiler_params=pltpu.CompilerParams(vmem_limit_bytes=VMEM),
        cost_estimate=pl.CostEstimate(flops=1, bytes_accessed=1, transcendentals=0),
        name="gate",
    )(*blocks, conv)


def local(qkv, short_filter, long_filter, skip, shard_doc, live):
    shards = lax.axis_size("ctx")
    halves = lax.axis_size("ch")
    here = lax.axis_index("ctx")
    mine = lax.axis_index("ch")
    tok, width = qkv.shape[1:]
    part = width // shards
    chips = shards // CORES
    span = chips // halves
    border = lax.ppermute(
        qkv[:, tok - 2 :, :], "ctx", [(i, i + 1) for i in range(shards - 1)]
    )
    filt = lax.dynamic_slice_in_dim(long_filter, here * part, part, axis=1)
    direct = lax.dynamic_slice_in_dim(skip, here * part, part, axis=0)[:, None]
    toeplitz = prepare(filt)
    out = jnp.zeros((halves, part, shards * tok // halves), jnp.bfloat16)

    def across(block, distance):
        return lax.ppermute(block, "ctx", [(i, i ^ distance) for i in range(shards)])

    (gated,) = short_convs(qkv, short_filter, shard_doc, live, (1, 2), False)
    gated = first_tokens(gated, qkv, border, short_filter, shard_doc, live)
    qkv, gated = lax.optimization_barrier((qkv, gated))
    queries = short_convs(qkv, short_filter, shard_doc, live, (0,), True, border)
    gated = lax.all_to_all(gated, "ctx", 0, 0)
    queries = [queries[0]] + [across(queries[k], k) for k in range(1, CORES)]
    queries = pair_up(queries)
    cuts = [0, span // 2, span * 3 // 4, span]
    groups = [
        [near + h * span for near in range(low, high) for h in reversed(range(halves))]
        for low, high in zip(cuts, cuts[1:])
    ]
    order = [far for fars in groups for far in fars if far]
    order = sorted(order, key=lambda far: far != 1)
    got = {0: queries[0]}

    def launch(fars, after):
        blocks, after = lax.optimization_barrier(([queries[far] for far in fars], after))
        for far, block in zip(fars, blocks):
            got[far] = across(block, far * CORES)
        return after

    early = [1, span]
    for far in early:
        got[far] = across(queries[far], far * CORES)
    order = [far for far in order if far not in early]
    middle = order[: 3 * len(order) // 5]
    gated, toeplitz = launch(middle, (gated, toeplitz))
    got[1], gated = lax.optimization_barrier((got[1], gated))
    conv = long_conv(gated, toeplitz, direct, shard_doc, live)
    conv = launch([far for far in order if far not in middle], conv)
    arrived = [[got[far] for far in fars] for fars in groups]
    for fars, blocks in zip(groups, arrived):
        own, sent = gate(fars, blocks, conv, halves)
        wide = own.shape[1]
        first = (here // CORES) % span ^ fars[-1]
        start = first // (len(fars) // halves) * wide
        out = lax.dynamic_update_slice(out, own[None], (mine, 0, start))
        for d in range(1, halves):
            route = [(j, (j + d) % halves) for j in range(halves)]
            came = lax.ppermute(sent[d - 1], "ch", route)
            source = lax.rem(mine + halves - d, halves)
            out = lax.dynamic_update_slice(out, came[None], (source, 0, start))
    return out


def solution(mesh):
    return jax.shard_map(
        local,
        mesh=mesh,
        in_specs=(P(None, "ctx", "ch"), P(None, None, "ch"), P(None, "ch"), P("ch"), P(), P()),
        out_specs=P(None, "ctx", "ch"),
        check_vma=False,
    )
```

```python
import functools

import jax
import jax.numpy as jnp
from jax import lax
from jax.experimental import pallas as pl
from jax.experimental.pallas import tpu as pltpu
from jax.sharding import PartitionSpec as P

LANES = 128
UNROLL = 8
ROWS = 64
CORES = 2
CHANS = 32
VMEM = 56 << 20


def shard_facts(doc, live, tok):
    shards = doc.shape[0]
    here = lax.axis_index("ctx")
    before = jnp.maximum(here - 1, 0)
    after = jnp.minimum(here + 1, shards - 1)
    joined = (here > 0) & (doc[before] == doc[here])
    closing = (here == shards - 1) | (doc[after] != doc[here])
    return joined, jnp.where(closing, live[here], tok)


def short_kernel(count, edges, doc, live, *refs):
    taps, slabs = refs[:count], refs[count : 2 * count]
    borders, refs = refs[2 * count : 2 * count + edges], refs[2 * count + edges :]
    outs, tall, turned = refs[:-2], refs[-2], refs[-1]
    here = lax.axis_index("ctx")
    tok = slabs[0].shape[1]
    joined, limit = shard_facts(doc, live, tok)

    def short(a):
        x = slabs[a][0].astype(jnp.float32)
        edge = jnp.zeros((2, x.shape[1]), jnp.float32)
        if edges:
            edge = jnp.where(joined, borders[a][0].astype(jnp.float32), 0.0)
        tall[a, 6:8, :] = edge
        tall[a, pl.ds(8, tok), :] = x
        once = tall[a, pl.ds(7, tok), :]
        twice = tall[a, pl.ds(6, tok), :]
        tap = taps[a]
        return tap[0, 0:1, :] * x + tap[0, 1:2, :] * once + tap[0, 2:3, :] * twice

    value = short(0)
    if count == 2:
        rows = lax.broadcasted_iota(jnp.int32, value.shape, 0)
        value = value * short(1) * jnp.where(rows < limit, 1.0, 0.0)
    value = value.astype(jnp.bfloat16).T
    if len(outs) == 1:
        part = outs[0].shape[1]
        for j in range(outs[0].shape[0]):
            outs[0][j] = value[j * part : (j + 1) * part]
    else:
        turned[...] = value
        part = outs[0].shape[1]
        for k, out in enumerate(outs):
            for j in range(out.shape[0]):
                row = (CORES * j + ((here % CORES) ^ k)) * part
                out[j] = turned[pl.ds(pl.multiple_of(row, part), part), :]


def short_convs(qkv, short_filter, shard_doc, live, which, split, border=None):
    _, tok, width = qkv.shape
    shards = shard_doc.shape[0]
    part = width // shards
    block = min(width, 512)
    smem = pl.BlockSpec(memory_space=pltpu.SMEM)
    count = len(which)
    borders = [] if border is None else [border] * count

    def spec(rows, a):
        return pl.BlockSpec((1, rows, block), lambda i: (a, 0, i))

    many = CORES if split else 1
    rows = block // part // many
    return pl.pallas_call(
        functools.partial(short_kernel, count, len(borders)),
        grid=(width // block,),
        in_specs=[smem] * 2
        + [spec(3, a) for a in which]
        + [spec(tok, a) for a in which]
        + [spec(2, a) for a in which if border is not None],
        out_specs=[pl.BlockSpec((rows, part, tok), lambda i: (i, 0, 0))] * many,
        out_shape=[jax.ShapeDtypeStruct((shards // many, part, tok), jnp.bfloat16)] * many,
        scratch_shapes=[
            pltpu.VMEM((count, tok + 8, block), jnp.float32),
            pltpu.VMEM((block, tok), jnp.bfloat16),
        ],
        compiler_params=pltpu.CompilerParams(vmem_limit_bytes=VMEM),
        name="short_" + "".join("qkv"[a] for a in which),
    )(shard_doc, live, *[short_filter] * count, *[qkv] * count, *borders)


def first_kernel(doc, live, key_edge, value_edge, key_taps, value_taps, key, value, old, out):
    shards, part, _ = old.shape
    tok = 2
    joined, limit = shard_facts(doc, live, tok)

    def short(edge, taps, slab):
        x = slab[0, :tok, :].astype(jnp.float32)
        edge = jnp.where(joined, edge[0].astype(jnp.float32), 0.0)
        once = jnp.concatenate([edge[1:], x[:1]], axis=0)
        return taps[0, 0:1, :] * x + taps[0, 1:2, :] * once + taps[0, 2:3, :] * edge

    keep = jnp.where(lax.broadcasted_iota(jnp.int32, (tok, 1), 0) < limit, 1.0, 0.0)
    both = short(key_edge, key_taps, key) * short(value_edge, value_taps, value) * keep
    tall = jnp.concatenate([both, jnp.zeros((LANES - tok, both.shape[1]), jnp.float32)], axis=0)
    new = tall.astype(jnp.bfloat16).T.reshape(shards, part, LANES)
    place = lax.broadcasted_iota(jnp.int32, new.shape, 2)
    out[...] = jnp.where(place < tok, new, old[...])


def first_tokens(gated, qkv, border, short_filter, shard_doc, live):
    shards, part, _ = gated.shape
    width = shards * part
    smem = pl.BlockSpec(memory_space=pltpu.SMEM)

    def spec(rows, a):
        return pl.BlockSpec((1, rows, width), lambda i: (a, 0, 0))

    tile = pl.BlockSpec((shards, part, LANES), lambda i: (0, 0, 0))
    return pl.pallas_call(
        first_kernel,
        grid=(1,),
        in_specs=[smem] * 2 + [spec(rows, a) for rows in (2, 3, 16) for a in (1, 2)] + [tile],
        out_specs=tile,
        out_shape=jax.ShapeDtypeStruct(gated.shape, gated.dtype),
        input_output_aliases={8: 0},
        compiler_params=pltpu.CompilerParams(vmem_limit_bytes=VMEM),
        name="first_tokens",
    )(shard_doc, live, *[border] * 2, *[short_filter] * 2, *[qkv] * 2, gated)


def pair_up_kernel(*refs):
    blocks, outs = refs[:CORES], refs[CORES:]
    here = lax.axis_index("ctx")
    for k, block in enumerate(blocks):
        row = (here % CORES) ^ k
        for far, out in enumerate(outs):
            out[row] = block[(here // CORES) ^ far]


def pair_up(blocks):
    chips, part, tok = blocks[0].shape
    vmem = pl.BlockSpec(memory_space=pltpu.VMEM)
    return pl.pallas_call(
        pair_up_kernel,
        in_specs=[vmem] * CORES,
        out_specs=[vmem] * chips,
        out_shape=[jax.ShapeDtypeStruct((CORES, part, tok), jnp.bfloat16)] * chips,
        compiler_params=pltpu.CompilerParams(vmem_limit_bytes=VMEM),
        name="pair_up",
    )(*blocks)


def prepare_kernel(filt, skip, out, column, taps):
    step = pl.program_id(0)
    chans, rows, width = out.shape

    @pl.when(step == 0)
    def _():
        taps[...] = filt[...].astype(jnp.float32).T

        column[...] = jnp.broadcast_to(skip[...], (8, skip.shape[1])).T[:, :1]

    def channel(c, _):
        row = taps[pl.ds(step * chans + c, 1), :]
        row = jnp.concatenate([row, jnp.zeros((1, width), jnp.float32)], axis=1)
        spread = jnp.broadcast_to(row, (16, row.shape[1]))
        band = pltpu.roll(spread, 0, 1, stride=1, stride_axis=0).astype(jnp.bfloat16)
        bands = [band] + [pltpu.roll(band, 16 * q, 1) for q in range(1, ROWS // 16)]
        toeplitz = jnp.concatenate(bands, axis=0)
        for k in range(rows // ROWS):
            out[c, k * ROWS : (k + 1) * ROWS, :] = toeplitz[:, k * width : (k + 1) * width]
        return 0

    lax.fori_loop(0, chans, channel, 0, unroll=4)


def prepare(filt, skip):
    lags, part = filt.shape
    chans = min(CHANS, part)
    width = 4 * ROWS
    rows = (lags // width + 1) * ROWS
    return pl.pallas_call(
        prepare_kernel,
        grid=(part // chans,),
        in_specs=[
            pl.BlockSpec((lags, part), lambda i: (0, 0)),
            pl.BlockSpec((1, part), lambda i: (0, 0)),
        ],
        out_specs=[
            pl.BlockSpec((chans, rows, width), lambda i: (i, 0, 0)),
            pl.BlockSpec((part, 1), lambda i: (0, 0)),
        ],
        out_shape=[
            jax.ShapeDtypeStruct((part, rows, width), jnp.bfloat16),
            jax.ShapeDtypeStruct((part, 1), jnp.float32),
        ],
        scratch_shapes=[pltpu.VMEM((part, lags), jnp.float32)],
        compiler_params=pltpu.CompilerParams(
            vmem_limit_bytes=VMEM, dimension_semantics=("arbitrary",)
        ),
        name="prepare",
    )(filt, skip[None, :])


def conv_kernel(doc, live, skip, toeplitz, gated, out, masks, wide, one, late, mixed):
    shards, chans, tok = gated.shape
    pitch = chans + 1
    per = tok // LANES
    fine = tok // ROWS
    blocks = shards * fine
    pairs = masks.shape[0] - 1
    pad = 8 * (pairs - 1)
    step = pl.program_id(0)
    depth = toeplitz.shape[1]

    @pl.when(step == 0)
    def _():
        wide[pl.ds(0, pad * pitch), :] = jnp.zeros((pad * pitch, LANES), jnp.float32)
        late[:, pl.ds(0, 8), :] = jnp.zeros((late.shape[0], 8, LANES), jnp.float32)
        start = jnp.int32(0)
        rows = lax.broadcasted_iota(jnp.int32, (fine, LANES), 0)
        left = lax.broadcasted_iota(jnp.int32, (blocks, LANES), 1) < ROWS
        runs = []
        for s in range(shards):
            if s > 0:
                start = jnp.where(doc[s] == doc[s - 1], start, s)
            runs.append(rows + (s - start) * fine)
        run = jnp.concatenate(runs, axis=0)
        for m in range(pairs):
            reach = jnp.where(left, 8 * m, 8 * m + 4)
            masks[m] = jnp.where(run >= reach, 1.0, 0.0).astype(jnp.bfloat16)
        masks[pairs] = jnp.where(run >= 2, 1.0, 0.0).astype(jnp.bfloat16)

    left = lax.broadcasted_iota(jnp.int32, (chans, LANES), 1) < ROWS
    older = [(jnp.zeros((chans, LANES), jnp.float32),) * 2] * 2
    for s in range(shards):
        for b in range(per):
            here = gated[s, :, b * LANES : (b + 1) * LANES].astype(jnp.float32)
            turned = pltpu.roll(here, ROWS, 1)
            row = pad + s * fine + 2 * b
            wide[pl.ds(row * pitch, chans), :] = jnp.where(left, here, older[0][1])
            wide[pl.ds((row + 1) * pitch, chans), :] = jnp.where(left, turned, older[0][0])
            older = [older[1], (here, turned)]

    def channel(c, slot):
        one[slot] = wide[pl.ds(c, blocks + pad, stride=pitch), :]
        lagged = [
            one[slot, pl.ds(pad - 8 * m, blocks), :].astype(jnp.bfloat16) * masks[m]
            for m in range(pairs)
        ]
        sums = jnp.dot(
            jnp.concatenate(lagged, axis=1)[:, :depth],
            toeplitz[c],
            preferred_element_type=jnp.float32,
        )
        late[slot, pl.ds(8, blocks), :] = sums[:, LANES:]
        behind = late[slot, pl.ds(6, blocks), :] * masks[pairs].astype(jnp.float32)
        mixed[pl.ds(c, blocks, stride=pitch), :] = sums[:, :LANES] + behind

    def group(i, _):
        for slot in range(UNROLL):
            channel(i * UNROLL + slot, slot)
        return 0

    lax.fori_loop(0, chans // UNROLL, group, 0)

    direct = skip[...]
    places = lax.broadcasted_iota(jnp.int32, (1, tok), 1)
    for s in range(shards):
        if s < shards - 1:
            limit = jnp.where(doc[s] != doc[s + 1], live[s], tok)
        else:
            limit = live[s]
        keep = jnp.where(places < limit, 1.0, 0.0)
        sums = []
        for b in range(per):
            row = s * fine + 2 * b
            after = mixed[pl.ds((row + 1) * pitch, chans), :]
            if row > 0:
                spill = mixed[pl.ds((row - 1) * pitch, chans), :]
                if b == 0:
                    spill = jnp.where(doc[s] == doc[s - 1], spill, 0.0)
            else:
                spill = jnp.zeros_like(after)
            sums.append(
                mixed[pl.ds(row * pitch, chans), :]
                + pltpu.roll(jnp.where(left, after, spill), ROWS, 1)
            )
        conv = jnp.concatenate(sums, axis=1)
        total = (conv + direct * gated[s].astype(jnp.float32)) * keep
        out[s] = total.astype(jnp.bfloat16)


def long_conv(gated, toeplitz, skip, shard_doc, live):
    shards, width, tok = gated.shape
    depth = toeplitz.shape[1]
    chans = min(CHANS, width)
    blocks = shards * tok // ROWS
    pairs = (depth // ROWS + 1) // 2
    tall = blocks + 8 * (pairs - 1)
    smem = pl.BlockSpec(memory_space=pltpu.SMEM)
    slab = pl.BlockSpec((shards, chans, tok), lambda i: (0, i, 0))
    return pl.pallas_call(
        conv_kernel,
        grid=(width // chans,),
        in_specs=[
            smem,
            smem,
            pl.BlockSpec((chans, 1), lambda i: (i, 0)),
            pl.BlockSpec((chans, depth, 4 * ROWS), lambda i: (i, 0, 0)),
            slab,
        ],
        out_specs=slab,
        out_shape=jax.ShapeDtypeStruct((shards, width, tok), jnp.bfloat16),
        scratch_shapes=[
            pltpu.VMEM((pairs + 1, blocks, LANES), jnp.bfloat16),
            pltpu.VMEM((tall * (chans + 1), LANES), jnp.float32),
            pltpu.VMEM((UNROLL, tall, LANES), jnp.float32),
            pltpu.VMEM((UNROLL, blocks + 8, LANES), jnp.float32),
            pltpu.VMEM((blocks * (chans + 1), LANES), jnp.float32),
        ],
        compiler_params=pltpu.CompilerParams(
            vmem_limit_bytes=VMEM, dimension_semantics=("arbitrary",)
        ),
        cost_estimate=pl.CostEstimate(flops=1, bytes_accessed=1, transcendentals=0),
        name="long_conv",
    )(shard_doc, live, skip, toeplitz, gated)


def gate_kernel(fars, *refs):
    blocks, conv, own, sent = refs[:-3], refs[-3], refs[-2], refs[-1]
    shards, _, tok = conv.shape
    halves = sent.shape[0] + 1
    per = shards // halves
    span = len(fars) // halves
    here = lax.axis_index("ctx")
    mine = lax.axis_index("ch")
    for far, block in zip(fars, blocks):
        chip = (here // CORES) ^ far
        first = chip * CORES
        away = (first // per + halves - mine) % halves
        values = [
            (block[k].astype(jnp.float32) * conv[first + k].astype(jnp.float32)).astype(
                jnp.bfloat16
            )
            for k in range(CORES)
        ]
        value = jnp.concatenate(values, axis=1)
        start = chip % span * (CORES * tok)
        column = pl.ds(pl.multiple_of(start, CORES * tok), CORES * tok)

        @pl.when(away == 0)
        def _():
            own[:, column] = value

        @pl.when(away != 0)
        def _():
            sent[away - 1, :, column] = value


def gate(fars, blocks, conv, halves):
    _, width, tok = blocks[0].shape
    shards = conv.shape[0]
    chans = min(64, width)
    wide = len(fars) // halves * CORES * tok
    return pl.pallas_call(
        functools.partial(gate_kernel, fars),
        grid=(width // chans,),
        in_specs=[pl.BlockSpec((CORES, chans, tok), lambda i: (0, i, 0))] * len(blocks)
        + [pl.BlockSpec((shards, chans, tok), lambda i: (0, i, 0))],
        out_specs=[
            pl.BlockSpec((chans, wide), lambda i: (i, 0)),
            pl.BlockSpec((halves - 1, chans, wide), lambda i: (0, i, 0)),
        ],
        out_shape=[
            jax.ShapeDtypeStruct((width, wide), jnp.bfloat16),
            jax.ShapeDtypeStruct((halves - 1, width, wide), jnp.bfloat16),
        ],
        compiler_params=pltpu.CompilerParams(vmem_limit_bytes=VMEM),
        cost_estimate=pl.CostEstimate(flops=1, bytes_accessed=1, transcendentals=0),
        name="gate",
    )(*blocks, conv)


def local(qkv, short_filter, long_filter, skip, shard_doc, live):
    shards = lax.axis_size("ctx")
    halves = lax.axis_size("ch")
    here = lax.axis_index("ctx")
    mine = lax.axis_index("ch")
    tok, width = qkv.shape[1:]
    part = width // shards
    chips = shards // CORES
    span = chips // halves
    border = lax.ppermute(
        qkv[:, tok - 2 :, :], "ctx", [(i, i + 1) for i in range(shards - 1)]
    )
    filt = lax.dynamic_slice_in_dim(long_filter, here * part, part, axis=1)
    direct = lax.dynamic_slice_in_dim(skip, here * part, part, axis=0)
    out = jnp.zeros((halves, part, shards * tok // halves), jnp.bfloat16)

    def across(block, distance):
        return lax.ppermute(block, "ctx", [(i, i ^ distance) for i in range(shards)])

    (gated,) = short_convs(qkv, short_filter, shard_doc, live, (1, 2), False)
    gated = first_tokens(gated, qkv, border, short_filter, shard_doc, live)
    qkv, gated = lax.optimization_barrier((qkv, gated))
    queries = short_convs(qkv, short_filter, shard_doc, live, (0,), True, border)
    gated = lax.all_to_all(gated, "ctx", 0, 0)
    queries = [queries[0]] + [across(queries[k], k) for k in range(1, CORES)]
    queries = pair_up(queries)
    cuts = [0, span // 2, span * 3 // 4, span]
    groups = [
        [near + h * span for near in range(low, high) for h in reversed(range(halves))]
        for low, high in zip(cuts, cuts[1:])
    ]
    order = [far for fars in groups for far in fars if far]
    order = sorted(order, key=lambda far: far != 1)
    got = {0: queries[0]}

    def launch(fars, after):
        blocks, after = lax.optimization_barrier(([queries[far] for far in fars], after))
        for far, block in zip(fars, blocks):
            got[far] = across(block, far * CORES)
        return after

    early = [1, span, span - 1]
    for far in early:
        got[far] = across(queries[far], far * CORES)
    got[1], filt = lax.optimization_barrier((got[1], filt))
    toeplitz, direct = prepare(filt, direct)
    order = [far for far in order if far not in early]
    order = sorted(order, key=lambda far: (far not in groups[0], far < span))
    last = [far for far in order if far in groups[2]]
    middle = [far for far in order if far not in last]
    late = last
    gated, toeplitz = launch(middle, (gated, toeplitz))
    got[1], gated = lax.optimization_barrier((got[1], gated))
    conv = long_conv(gated, toeplitz, direct, shard_doc, live)
    for fars in groups:
        own, sent = gate(fars, [got[far] for far in fars], conv, halves)
        if late:
            sent = launch(late, sent)
            late = []
        wide = own.shape[1]
        first = (here // CORES) % span ^ fars[-1]
        start = first // (len(fars) // halves) * wide
        out = lax.dynamic_update_slice(out, own[None], (mine, 0, start))
        for d in range(1, halves):
            route = [(j, (j + d) % halves) for j in range(halves)]
            came = lax.ppermute(sent[d - 1], "ch", route)
            source = lax.rem(mine + halves - d, halves)
            out = lax.dynamic_update_slice(out, came[None], (source, 0, start))
    return out


def solution(mesh):
    return jax.shard_map(
        local,
        mesh=mesh,
        in_specs=(P(None, "ctx", "ch"), P(None, None, "ch"), P(None, "ch"), P("ch"), P(), P()),
        out_specs=P(None, "ctx", "ch"),
        check_vma=False,
    )
```

```python
import functools

import jax
import jax.numpy as jnp
from jax import lax
from jax.experimental import pallas as pl
from jax.experimental.pallas import tpu as pltpu
from jax.sharding import PartitionSpec as P

LANES = 128
UNROLL = 16
ROWS = 64
CORES = 2
CHANS = 32
VMEM = 56 << 20


def shard_facts(doc, live, tok):
    shards = doc.shape[0]
    here = lax.axis_index("ctx")
    before = jnp.maximum(here - 1, 0)
    after = jnp.minimum(here + 1, shards - 1)
    joined = (here > 0) & (doc[before] == doc[here])
    closing = (here == shards - 1) | (doc[after] != doc[here])
    return joined, jnp.where(closing, live[here], tok)


def short_kernel(count, edges, doc, live, *refs):
    taps, slabs = refs[:count], refs[count : 2 * count]
    borders, refs = refs[2 * count : 2 * count + edges], refs[2 * count + edges :]
    outs, tall, turned = refs[:-2], refs[-2], refs[-1]
    here = lax.axis_index("ctx")
    tok = slabs[0].shape[1]
    joined, limit = shard_facts(doc, live, tok)

    def short(a):
        x = slabs[a][0].astype(jnp.float32)
        edge = jnp.zeros((2, x.shape[1]), jnp.float32)
        if edges:
            edge = jnp.where(joined, borders[a][0].astype(jnp.float32), 0.0)
        tall[a, 6:8, :] = edge
        tall[a, pl.ds(8, tok), :] = x
        once = tall[a, pl.ds(7, tok), :]
        twice = tall[a, pl.ds(6, tok), :]
        tap = taps[a]
        return tap[0, 0:1, :] * x + tap[0, 1:2, :] * once + tap[0, 2:3, :] * twice

    value = short(0)
    if count == 2:
        rows = lax.broadcasted_iota(jnp.int32, value.shape, 0)
        value = value * short(1) * jnp.where(rows < limit, 1.0, 0.0)
    value = value.astype(jnp.bfloat16).T
    if len(outs) == 1:
        part = outs[0].shape[1]
        for j in range(outs[0].shape[0]):
            outs[0][j] = value[j * part : (j + 1) * part]
    else:
        turned[...] = value
        part = outs[0].shape[1]
        for k, out in enumerate(outs):
            for j in range(out.shape[0]):
                row = (CORES * j + ((here % CORES) ^ k)) * part
                out[j] = turned[pl.ds(pl.multiple_of(row, part), part), :]


def short_convs(qkv, short_filter, shard_doc, live, which, split, border=None):
    _, tok, width = qkv.shape
    shards = shard_doc.shape[0]
    part = width // shards
    block = min(width, 512)
    smem = pl.BlockSpec(memory_space=pltpu.SMEM)
    count = len(which)
    borders = [] if border is None else [border] * count

    def spec(rows, a):
        return pl.BlockSpec((1, rows, block), lambda i: (a, 0, i))

    many = CORES if split else 1
    rows = block // part // many
    return pl.pallas_call(
        functools.partial(short_kernel, count, len(borders)),
        grid=(width // block,),
        in_specs=[smem] * 2
        + [spec(3, a) for a in which]
        + [spec(tok, a) for a in which]
        + [spec(2, a) for a in which if border is not None],
        out_specs=[pl.BlockSpec((rows, part, tok), lambda i: (i, 0, 0))] * many,
        out_shape=[jax.ShapeDtypeStruct((shards // many, part, tok), jnp.bfloat16)] * many,
        scratch_shapes=[
            pltpu.VMEM((count, tok + 8, block), jnp.float32),
            pltpu.VMEM((block, tok), jnp.bfloat16),
        ],
        compiler_params=pltpu.CompilerParams(vmem_limit_bytes=VMEM),
        name="short_" + "".join("qkv"[a] for a in which),
    )(shard_doc, live, *[short_filter] * count, *[qkv] * count, *borders)


def first_kernel(doc, live, key_edge, value_edge, key_taps, value_taps, key, value, old, out):
    shards, part, _ = old.shape
    tok = 2
    joined, limit = shard_facts(doc, live, tok)

    def short(edge, taps, slab):
        x = slab[0, :tok, :].astype(jnp.float32)
        edge = jnp.where(joined, edge[0].astype(jnp.float32), 0.0)
        once = jnp.concatenate([edge[1:], x[:1]], axis=0)
        return taps[0, 0:1, :] * x + taps[0, 1:2, :] * once + taps[0, 2:3, :] * edge

    keep = jnp.where(lax.broadcasted_iota(jnp.int32, (tok, 1), 0) < limit, 1.0, 0.0)
    both = short(key_edge, key_taps, key) * short(value_edge, value_taps, value) * keep
    tall = jnp.concatenate([both, jnp.zeros((LANES - tok, both.shape[1]), jnp.float32)], axis=0)
    new = tall.astype(jnp.bfloat16).T.reshape(shards, part, LANES)
    place = lax.broadcasted_iota(jnp.int32, new.shape, 2)
    out[...] = jnp.where(place < tok, new, old[...])


def first_tokens(gated, qkv, border, short_filter, shard_doc, live):
    shards, part, _ = gated.shape
    width = shards * part
    smem = pl.BlockSpec(memory_space=pltpu.SMEM)

    def spec(rows, a):
        return pl.BlockSpec((1, rows, width), lambda i: (a, 0, 0))

    tile = pl.BlockSpec((shards, part, LANES), lambda i: (0, 0, 0))
    return pl.pallas_call(
        first_kernel,
        grid=(1,),
        in_specs=[smem] * 2 + [spec(rows, a) for rows in (2, 3, 16) for a in (1, 2)] + [tile],
        out_specs=tile,
        out_shape=jax.ShapeDtypeStruct(gated.shape, gated.dtype),
        input_output_aliases={8: 0},
        compiler_params=pltpu.CompilerParams(vmem_limit_bytes=VMEM),
        name="first_tokens",
    )(shard_doc, live, *[border] * 2, *[short_filter] * 2, *[qkv] * 2, gated)


def pair_up_kernel(*refs):
    blocks, outs = refs[:CORES], refs[CORES:]
    here = lax.axis_index("ctx")
    for k, block in enumerate(blocks):
        row = (here % CORES) ^ k
        for far, out in enumerate(outs):
            out[row] = block[(here // CORES) ^ far]


def pair_up(blocks):
    chips, part, tok = blocks[0].shape
    vmem = pl.BlockSpec(memory_space=pltpu.VMEM)
    return pl.pallas_call(
        pair_up_kernel,
        in_specs=[vmem] * CORES,
        out_specs=[vmem] * chips,
        out_shape=[jax.ShapeDtypeStruct((CORES, part, tok), jnp.bfloat16)] * chips,
        compiler_params=pltpu.CompilerParams(vmem_limit_bytes=VMEM),
        name="pair_up",
    )(*blocks)


def prepare_kernel(filt, skip, out, column, taps):
    step = pl.program_id(0)
    chans, rows, width = out.shape

    @pl.when(step == 0)
    def _():
        taps[...] = filt[...].astype(jnp.float32).T

        column[...] = jnp.broadcast_to(skip[...], (8, skip.shape[1])).T[:, :1]

    def channel(c, _):
        row = taps[pl.ds(step * chans + c, 1), :]
        row = jnp.concatenate([row, jnp.zeros((1, width), jnp.float32)], axis=1)
        spread = jnp.broadcast_to(row, (16, row.shape[1]))
        band = pltpu.roll(spread, 0, 1, stride=1, stride_axis=0).astype(jnp.bfloat16)
        bands = [band] + [pltpu.roll(band, 16 * q, 1) for q in range(1, ROWS // 16)]
        toeplitz = jnp.concatenate(bands, axis=0)
        for k in range(rows // ROWS):
            out[c, k * ROWS : (k + 1) * ROWS, :] = toeplitz[:, k * width : (k + 1) * width]
        return 0

    lax.fori_loop(0, chans, channel, 0, unroll=8)


def prepare(filt, skip):
    lags, part = filt.shape
    chans = min(CHANS, part)
    width = 4 * ROWS
    rows = (lags // width + 1) * ROWS
    return pl.pallas_call(
        prepare_kernel,
        grid=(part // chans,),
        in_specs=[
            pl.BlockSpec((lags, part), lambda i: (0, 0)),
            pl.BlockSpec((1, part), lambda i: (0, 0)),
        ],
        out_specs=[
            pl.BlockSpec((chans, rows, width), lambda i: (i, 0, 0)),
            pl.BlockSpec((part, 1), lambda i: (0, 0)),
        ],
        out_shape=[
            jax.ShapeDtypeStruct((part, rows, width), jnp.bfloat16),
            jax.ShapeDtypeStruct((part, 1), jnp.float32),
        ],
        scratch_shapes=[pltpu.VMEM((part, lags), jnp.float32)],
        compiler_params=pltpu.CompilerParams(
            vmem_limit_bytes=VMEM, dimension_semantics=("arbitrary",)
        ),
        name="prepare",
    )(filt, skip[None, :])


def conv_kernel(doc, live, skip, toeplitz, gated, out, masks, wide, one, late, mixed):
    shards, chans, tok = gated.shape
    pitch = chans + 1
    per = tok // LANES
    fine = tok // ROWS
    blocks = shards * fine
    pairs = masks.shape[0] - 1
    pad = 8 * (pairs - 1)
    step = pl.program_id(0)
    depth = toeplitz.shape[1]

    @pl.when(step == 0)
    def _():
        wide[pl.ds(0, pad * pitch), :] = jnp.zeros((pad * pitch, LANES), jnp.float32)
        late[:, pl.ds(0, 8), :] = jnp.zeros((late.shape[0], 8, LANES), jnp.float32)
        start = jnp.int32(0)
        rows = lax.broadcasted_iota(jnp.int32, (fine, LANES), 0)
        left = lax.broadcasted_iota(jnp.int32, (blocks, LANES), 1) < ROWS
        runs = []
        for s in range(shards):
            if s > 0:
                start = jnp.where(doc[s] == doc[s - 1], start, s)
            runs.append(rows + (s - start) * fine)
        run = jnp.concatenate(runs, axis=0)
        for m in range(pairs):
            reach = jnp.where(left, 8 * m, 8 * m + 4)
            masks[m] = jnp.where(run >= reach, 1.0, 0.0).astype(jnp.bfloat16)
        masks[pairs] = jnp.where(run >= 2, 1.0, 0.0).astype(jnp.bfloat16)

    left = lax.broadcasted_iota(jnp.int32, (chans, LANES), 1) < ROWS
    older = [(jnp.zeros((chans, LANES), jnp.float32),) * 2] * 2
    for s in range(shards):
        for b in range(per):
            here = gated[s, :, b * LANES : (b + 1) * LANES].astype(jnp.float32)
            turned = pltpu.roll(here, ROWS, 1)
            row = pad + s * fine + 2 * b
            wide[pl.ds(row * pitch, chans), :] = jnp.where(left, here, older[0][1])
            wide[pl.ds((row + 1) * pitch, chans), :] = jnp.where(left, turned, older[0][0])
            older = [older[1], (here, turned)]

    def channel(c, slot):
        one[slot] = wide[pl.ds(c, blocks + pad, stride=pitch), :]
        lagged = [
            one[slot, pl.ds(pad - 8 * m, blocks), :].astype(jnp.bfloat16) * masks[m]
            for m in range(pairs)
        ]
        sums = jnp.dot(
            jnp.concatenate(lagged, axis=1)[:, :depth],
            toeplitz[c],
            preferred_element_type=jnp.float32,
        )
        late[slot, pl.ds(8, blocks), :] = sums[:, LANES:]
        behind = late[slot, pl.ds(6, blocks), :] * masks[pairs].astype(jnp.float32)
        mixed[pl.ds(c, blocks, stride=pitch), :] = sums[:, :LANES] + behind

    def group(i, _):
        for slot in range(UNROLL):
            channel(i * UNROLL + slot, slot)
        return 0

    lax.fori_loop(0, chans // UNROLL, group, 0)

    direct = skip[...]
    places = lax.broadcasted_iota(jnp.int32, (1, tok), 1)
    for s in range(shards):
        if s < shards - 1:
            limit = jnp.where(doc[s] != doc[s + 1], live[s], tok)
        else:
            limit = live[s]
        keep = jnp.where(places < limit, 1.0, 0.0)
        sums = []
        for b in range(per):
            row = s * fine + 2 * b
            after = mixed[pl.ds((row + 1) * pitch, chans), :]
            if row > 0:
                spill = mixed[pl.ds((row - 1) * pitch, chans), :]
                if b == 0:
                    spill = jnp.where(doc[s] == doc[s - 1], spill, 0.0)
            else:
                spill = jnp.zeros_like(after)
            sums.append(
                mixed[pl.ds(row * pitch, chans), :]
                + pltpu.roll(jnp.where(left, after, spill), ROWS, 1)
            )
        conv = jnp.concatenate(sums, axis=1)
        total = (conv + direct * gated[s].astype(jnp.float32)) * keep
        out[s] = total.astype(jnp.bfloat16)


def long_conv(gated, toeplitz, skip, shard_doc, live):
    shards, width, tok = gated.shape
    depth = toeplitz.shape[1]
    chans = min(CHANS, width)
    blocks = shards * tok // ROWS
    pairs = (depth // ROWS + 1) // 2
    tall = blocks + 8 * (pairs - 1)
    smem = pl.BlockSpec(memory_space=pltpu.SMEM)
    slab = pl.BlockSpec((shards, chans, tok), lambda i: (0, i, 0))
    return pl.pallas_call(
        conv_kernel,
        grid=(width // chans,),
        in_specs=[
            smem,
            smem,
            pl.BlockSpec((chans, 1), lambda i: (i, 0)),
            pl.BlockSpec((chans, depth, 4 * ROWS), lambda i: (i, 0, 0)),
            slab,
        ],
        out_specs=slab,
        out_shape=jax.ShapeDtypeStruct((shards, width, tok), jnp.bfloat16),
        scratch_shapes=[
            pltpu.VMEM((pairs + 1, blocks, LANES), jnp.bfloat16),
            pltpu.VMEM((tall * (chans + 1), LANES), jnp.float32),
            pltpu.VMEM((UNROLL, tall, LANES), jnp.float32),
            pltpu.VMEM((UNROLL, blocks + 8, LANES), jnp.float32),
            pltpu.VMEM((blocks * (chans + 1), LANES), jnp.float32),
        ],
        compiler_params=pltpu.CompilerParams(
            vmem_limit_bytes=VMEM, dimension_semantics=("arbitrary",)
        ),
        cost_estimate=pl.CostEstimate(flops=1, bytes_accessed=1, transcendentals=0),
        name="long_conv",
    )(shard_doc, live, skip, toeplitz, gated)


def gate_kernel(fars, *refs):
    blocks, conv, own, sent = refs[:-3], refs[-3], refs[-2], refs[-1]
    shards, _, tok = conv.shape
    halves = sent.shape[0] + 1
    per = shards // halves
    span = len(fars) // halves
    here = lax.axis_index("ctx")
    mine = lax.axis_index("ch")
    for far, block in zip(fars, blocks):
        chip = (here // CORES) ^ far
        first = chip * CORES
        away = (first // per + halves - mine) % halves
        values = [
            (block[k].astype(jnp.float32) * conv[first + k].astype(jnp.float32)).astype(
                jnp.bfloat16
            )
            for k in range(CORES)
        ]
        value = jnp.concatenate(values, axis=1)
        start = chip % span * (CORES * tok)
        column = pl.ds(pl.multiple_of(start, CORES * tok), CORES * tok)

        @pl.when(away == 0)
        def _():
            own[:, column] = value

        @pl.when(away != 0)
        def _():
            sent[away - 1, :, column] = value


def gate(fars, blocks, conv, halves):
    _, width, tok = blocks[0].shape
    shards = conv.shape[0]
    chans = min(64, width)
    wide = len(fars) // halves * CORES * tok
    return pl.pallas_call(
        functools.partial(gate_kernel, fars),
        grid=(width // chans,),
        in_specs=[pl.BlockSpec((CORES, chans, tok), lambda i: (0, i, 0))] * len(blocks)
        + [pl.BlockSpec((shards, chans, tok), lambda i: (0, i, 0))],
        out_specs=[
            pl.BlockSpec((chans, wide), lambda i: (i, 0)),
            pl.BlockSpec((halves - 1, chans, wide), lambda i: (0, i, 0)),
        ],
        out_shape=[
            jax.ShapeDtypeStruct((width, wide), jnp.bfloat16),
            jax.ShapeDtypeStruct((halves - 1, width, wide), jnp.bfloat16),
        ],
        compiler_params=pltpu.CompilerParams(vmem_limit_bytes=VMEM),
        cost_estimate=pl.CostEstimate(flops=1, bytes_accessed=1, transcendentals=0),
        name="gate",
    )(*blocks, conv)


def local(qkv, short_filter, long_filter, skip, shard_doc, live):
    shards = lax.axis_size("ctx")
    halves = lax.axis_size("ch")
    here = lax.axis_index("ctx")
    mine = lax.axis_index("ch")
    tok, width = qkv.shape[1:]
    part = width // shards
    chips = shards // CORES
    span = chips // halves
    border = lax.ppermute(
        qkv[:, tok - 2 :, :], "ctx", [(i, i + 1) for i in range(shards - 1)]
    )
    filt = lax.dynamic_slice_in_dim(long_filter, here * part, part, axis=1)
    direct = lax.dynamic_slice_in_dim(skip, here * part, part, axis=0)
    out = jnp.zeros((halves, part, shards * tok // halves), jnp.bfloat16)

    def across(block, distance):
        return lax.ppermute(block, "ctx", [(i, i ^ distance) for i in range(shards)])

    (gated,) = short_convs(qkv, short_filter, shard_doc, live, (1, 2), False)
    gated = first_tokens(gated, qkv, border, short_filter, shard_doc, live)
    qkv, gated = lax.optimization_barrier((qkv, gated))
    queries = short_convs(qkv, short_filter, shard_doc, live, (0,), True, border)
    gated = lax.all_to_all(gated, "ctx", 0, 0)
    queries = [queries[0]] + [across(queries[k], k) for k in range(1, CORES)]
    queries = pair_up(queries)
    cuts = [0, span // 4, span // 2, span * 3 // 4, span]
    groups = [
        [near + h * span for near in range(low, high) for h in reversed(range(halves))]
        for low, high in zip(cuts, cuts[1:])
    ]
    order = [far for fars in groups for far in fars if far]
    order = sorted(order, key=lambda far: far != 1)
    got = {0: queries[0]}

    def launch(fars, after):
        blocks, after = lax.optimization_barrier(([queries[far] for far in fars], after))
        for far, block in zip(fars, blocks):
            got[far] = across(block, far * CORES)
        return after

    early = [1, span, span - 1]
    for far in early:
        got[far] = across(queries[far], far * CORES)
    got[1], filt = lax.optimization_barrier((got[1], filt))
    toeplitz, direct = prepare(filt, direct)
    order = [far for far in order if far not in early]
    order = sorted(order, key=lambda far: (far not in groups[0] + groups[1], far < span))
    last = [far for far in order if far in groups[-1]]
    middle = [far for far in order if far not in last]
    late = last
    gated, toeplitz = launch(middle, (gated, toeplitz))
    got[1], gated = lax.optimization_barrier((got[1], gated))
    conv = long_conv(gated, toeplitz, direct, shard_doc, live)
    for fars in groups:
        own, sent = gate(fars, [got[far] for far in fars], conv, halves)
        if late:
            sent = launch(late, sent)
            late = []
        wide = own.shape[1]
        first = (here // CORES) % span ^ fars[-1]
        start = first // (len(fars) // halves) * wide
        out = lax.dynamic_update_slice(out, own[None], (mine, 0, start))
        for d in range(1, halves):
            route = [(j, (j + d) % halves) for j in range(halves)]
            came = lax.ppermute(sent[d - 1], "ch", route)
            source = lax.rem(mine + halves - d, halves)
            out = lax.dynamic_update_slice(out, came[None], (source, 0, start))
    return out


def solution(mesh):
    return jax.shard_map(
        local,
        mesh=mesh,
        in_specs=(P(None, "ctx", "ch"), P(None, None, "ch"), P(None, "ch"), P("ch"), P(), P()),
        out_specs=P(None, "ctx", "ch"),
        check_vma=False,
    )
```

```python
import functools

import jax
import jax.numpy as jnp
from jax import lax
from jax.experimental import pallas as pl
from jax.experimental.pallas import tpu as pltpu
from jax.sharding import PartitionSpec as P

LANES = 128
UNROLL = 16
ROWS = 64
CORES = 2
CHANS = 32
VMEM = 56 << 20


def shard_facts(doc, live, tok):
    shards = doc.shape[0]
    here = lax.axis_index("ctx")
    before = jnp.maximum(here - 1, 0)
    after = jnp.minimum(here + 1, shards - 1)
    joined = (here > 0) & (doc[before] == doc[here])
    closing = (here == shards - 1) | (doc[after] != doc[here])
    return joined, jnp.where(closing, live[here], tok)


def short_kernel(count, edges, doc, live, *refs):
    taps, slabs = refs[:count], refs[count : 2 * count]
    borders, refs = refs[2 * count : 2 * count + edges], refs[2 * count + edges :]
    outs, tall, turned = refs[:-2], refs[-2], refs[-1]
    here = lax.axis_index("ctx")
    tok = slabs[0].shape[1]
    joined, limit = shard_facts(doc, live, tok)

    def short(a):
        x = slabs[a][0].astype(jnp.float32)
        edge = jnp.zeros((2, x.shape[1]), jnp.float32)
        if edges:
            edge = jnp.where(joined, borders[a][0].astype(jnp.float32), 0.0)
        tall[a, 6:8, :] = edge
        tall[a, pl.ds(8, tok), :] = x
        once = tall[a, pl.ds(7, tok), :]
        twice = tall[a, pl.ds(6, tok), :]
        tap = taps[a]
        return tap[0, 0:1, :] * x + tap[0, 1:2, :] * once + tap[0, 2:3, :] * twice

    value = short(0)
    if count == 2:
        rows = lax.broadcasted_iota(jnp.int32, value.shape, 0)
        value = value * short(1) * jnp.where(rows < limit, 1.0, 0.0)
    value = value.astype(jnp.bfloat16).T
    if len(outs) == 1:
        part = outs[0].shape[1]
        for j in range(outs[0].shape[0]):
            outs[0][j] = value[j * part : (j + 1) * part]
    else:
        turned[...] = value
        part = outs[0].shape[1]
        for k, out in enumerate(outs):
            for j in range(out.shape[0]):
                row = (CORES * j + ((here % CORES) ^ k)) * part
                out[j] = turned[pl.ds(pl.multiple_of(row, part), part), :]


def short_convs(qkv, short_filter, shard_doc, live, which, split, border=None):
    _, tok, width = qkv.shape
    shards = shard_doc.shape[0]
    part = width // shards
    block = min(width, 512)
    smem = pl.BlockSpec(memory_space=pltpu.SMEM)
    count = len(which)
    borders = [] if border is None else [border] * count

    def spec(rows, a):
        return pl.BlockSpec((1, rows, block), lambda i: (a, 0, i))

    many = CORES if split else 1
    rows = block // part // many
    return pl.pallas_call(
        functools.partial(short_kernel, count, len(borders)),
        grid=(width // block,),
        in_specs=[smem] * 2
        + [spec(3, a) for a in which]
        + [spec(tok, a) for a in which]
        + [spec(2, a) for a in which if border is not None],
        out_specs=[pl.BlockSpec((rows, part, tok), lambda i: (i, 0, 0))] * many,
        out_shape=[jax.ShapeDtypeStruct((shards // many, part, tok), jnp.bfloat16)] * many,
        scratch_shapes=[
            pltpu.VMEM((count, tok + 8, block), jnp.float32),
            pltpu.VMEM((block, tok), jnp.bfloat16),
        ],
        compiler_params=pltpu.CompilerParams(vmem_limit_bytes=VMEM),
        name="short_" + "".join("qkv"[a] for a in which),
    )(shard_doc, live, *[short_filter] * count, *[qkv] * count, *borders)


def first_kernel(doc, live, key_edge, value_edge, key_taps, value_taps, key, value, old, out):
    shards, part, _ = old.shape
    tok = 2
    joined, limit = shard_facts(doc, live, tok)

    def short(edge, taps, slab):
        x = slab[0, :tok, :].astype(jnp.float32)
        edge = jnp.where(joined, edge[0].astype(jnp.float32), 0.0)
        once = jnp.concatenate([edge[1:], x[:1]], axis=0)
        return taps[0, 0:1, :] * x + taps[0, 1:2, :] * once + taps[0, 2:3, :] * edge

    keep = jnp.where(lax.broadcasted_iota(jnp.int32, (tok, 1), 0) < limit, 1.0, 0.0)
    both = short(key_edge, key_taps, key) * short(value_edge, value_taps, value) * keep
    tall = jnp.concatenate([both, jnp.zeros((LANES - tok, both.shape[1]), jnp.float32)], axis=0)
    new = tall.astype(jnp.bfloat16).T.reshape(shards, part, LANES)
    place = lax.broadcasted_iota(jnp.int32, new.shape, 2)
    out[...] = jnp.where(place < tok, new, old[...])


def first_tokens(gated, qkv, border, short_filter, shard_doc, live):
    shards, part, _ = gated.shape
    width = shards * part
    smem = pl.BlockSpec(memory_space=pltpu.SMEM)

    def spec(rows, a):
        return pl.BlockSpec((1, rows, width), lambda i: (a, 0, 0))

    tile = pl.BlockSpec((shards, part, LANES), lambda i: (0, 0, 0))
    return pl.pallas_call(
        first_kernel,
        grid=(1,),
        in_specs=[smem] * 2 + [spec(rows, a) for rows in (2, 3, 16) for a in (1, 2)] + [tile],
        out_specs=tile,
        out_shape=jax.ShapeDtypeStruct(gated.shape, gated.dtype),
        input_output_aliases={8: 0},
        compiler_params=pltpu.CompilerParams(vmem_limit_bytes=VMEM),
        name="first_tokens",
    )(shard_doc, live, *[border] * 2, *[short_filter] * 2, *[qkv] * 2, gated)


def pair_up_kernel(*refs):
    blocks, outs = refs[:CORES], refs[CORES:]
    here = lax.axis_index("ctx")
    for k, block in enumerate(blocks):
        row = (here % CORES) ^ k
        for far, out in enumerate(outs):
            out[row] = block[(here // CORES) ^ far]


def pair_up(blocks):
    chips, part, tok = blocks[0].shape
    vmem = pl.BlockSpec(memory_space=pltpu.VMEM)
    return pl.pallas_call(
        pair_up_kernel,
        in_specs=[vmem] * CORES,
        out_specs=[vmem] * chips,
        out_shape=[jax.ShapeDtypeStruct((CORES, part, tok), jnp.bfloat16)] * chips,
        compiler_params=pltpu.CompilerParams(vmem_limit_bytes=VMEM),
        name="pair_up",
    )(*blocks)


def prepare_kernel(filt, skip, out, column, taps):
    step = pl.program_id(0)
    chans, rows, width = out.shape

    @pl.when(step == 0)
    def _():
        taps[...] = filt[...].astype(jnp.float32).T

        column[...] = jnp.broadcast_to(skip[...], (8, skip.shape[1])).T[:, :1]

    def channel(c, _):
        row = taps[pl.ds(step * chans + c, 1), :]
        row = jnp.concatenate([row, jnp.zeros((1, width), jnp.float32)], axis=1)
        spread = jnp.broadcast_to(row, (16, row.shape[1]))
        band = pltpu.roll(spread, 0, 1, stride=1, stride_axis=0).astype(jnp.bfloat16)
        bands = [band] + [pltpu.roll(band, 16 * q, 1) for q in range(1, ROWS // 16)]
        toeplitz = jnp.concatenate(bands, axis=0)
        for k in range(rows // ROWS):
            out[c, k * ROWS : (k + 1) * ROWS, :] = toeplitz[:, k * width : (k + 1) * width]
        return 0

    lax.fori_loop(0, chans, channel, 0, unroll=8)


def prepare(filt, skip):
    lags, part = filt.shape
    chans = min(CHANS, part)
    width = 4 * ROWS
    rows = (lags // width + 1) * ROWS
    return pl.pallas_call(
        prepare_kernel,
        grid=(part // chans,),
        in_specs=[
            pl.BlockSpec((lags, part), lambda i: (0, 0)),
            pl.BlockSpec((1, part), lambda i: (0, 0)),
        ],
        out_specs=[
            pl.BlockSpec((chans, rows, width), lambda i: (i, 0, 0)),
            pl.BlockSpec((part, 1), lambda i: (0, 0)),
        ],
        out_shape=[
            jax.ShapeDtypeStruct((part, rows, width), jnp.bfloat16),
            jax.ShapeDtypeStruct((part, 1), jnp.float32),
        ],
        scratch_shapes=[pltpu.VMEM((part, lags), jnp.float32)],
        compiler_params=pltpu.CompilerParams(
            vmem_limit_bytes=VMEM, dimension_semantics=("arbitrary",)
        ),
        name="prepare",
    )(filt, skip[None, :])


def conv_kernel(doc, live, skip, toeplitz, gated, out, masks, wide, one, late, mixed):
    shards, chans, tok = gated.shape
    pitch = chans + 1
    per = tok // LANES
    fine = tok // ROWS
    blocks = shards * fine
    pairs = masks.shape[0] - 1
    pad = 8 * (pairs - 1)
    step = pl.program_id(0)
    depth = toeplitz.shape[1]

    @pl.when(step == 0)
    def _():
        wide[pl.ds(0, pad * pitch), :] = jnp.zeros((pad * pitch, LANES), jnp.float32)
        late[:, pl.ds(0, 8), :] = jnp.zeros((late.shape[0], 8, LANES), jnp.float32)
        start = jnp.int32(0)
        rows = lax.broadcasted_iota(jnp.int32, (fine, LANES), 0)
        left = lax.broadcasted_iota(jnp.int32, (blocks, LANES), 1) < ROWS
        runs = []
        for s in range(shards):
            if s > 0:
                start = jnp.where(doc[s] == doc[s - 1], start, s)
            runs.append(rows + (s - start) * fine)
        run = jnp.concatenate(runs, axis=0)
        for m in range(pairs):
            reach = jnp.where(left, 8 * m, 8 * m + 4)
            masks[m] = jnp.where(run >= reach, 1.0, 0.0).astype(jnp.bfloat16)
        masks[pairs] = jnp.where(run >= 2, 1.0, 0.0).astype(jnp.bfloat16)

    left = lax.broadcasted_iota(jnp.int32, (chans, LANES), 1) < ROWS
    older = [(jnp.zeros((chans, LANES), jnp.float32),) * 2] * 2
    for s in range(shards):
        for b in range(per):
            here = gated[s, :, b * LANES : (b + 1) * LANES].astype(jnp.float32)
            turned = pltpu.roll(here, ROWS, 1)
            row = pad + s * fine + 2 * b
            wide[pl.ds(row * pitch, chans), :] = jnp.where(left, here, older[0][1])
            wide[pl.ds((row + 1) * pitch, chans), :] = jnp.where(left, turned, older[0][0])
            older = [older[1], (here, turned)]

    def channel(c, slot):
        one[slot] = wide[pl.ds(c, blocks + pad, stride=pitch), :]
        lagged = [
            one[slot, pl.ds(pad - 8 * m, blocks), :].astype(jnp.bfloat16) * masks[m]
            for m in range(pairs)
        ]
        sums = jnp.dot(
            jnp.concatenate(lagged, axis=1)[:, :depth],
            toeplitz[c],
            preferred_element_type=jnp.float32,
        )
        late[slot, pl.ds(8, blocks), :] = sums[:, LANES:]
        behind = late[slot, pl.ds(6, blocks), :] * masks[pairs].astype(jnp.float32)
        mixed[pl.ds(c, blocks, stride=pitch), :] = sums[:, :LANES] + behind

    def group(i, _):
        for slot in range(UNROLL):
            channel(i * UNROLL + slot, slot)
        return 0

    lax.fori_loop(0, chans // UNROLL, group, 0)

    direct = skip[...]
    places = lax.broadcasted_iota(jnp.int32, (1, tok), 1)
    for s in range(shards):
        if s < shards - 1:
            limit = jnp.where(doc[s] != doc[s + 1], live[s], tok)
        else:
            limit = live[s]
        keep = jnp.where(places < limit, 1.0, 0.0)
        sums = []
        for b in range(per):
            row = s * fine + 2 * b
            after = mixed[pl.ds((row + 1) * pitch, chans), :]
            if row > 0:
                spill = mixed[pl.ds((row - 1) * pitch, chans), :]
                if b == 0:
                    spill = jnp.where(doc[s] == doc[s - 1], spill, 0.0)
            else:
                spill = jnp.zeros_like(after)
            sums.append(
                mixed[pl.ds(row * pitch, chans), :]
                + pltpu.roll(jnp.where(left, after, spill), ROWS, 1)
            )
        conv = jnp.concatenate(sums, axis=1)
        total = (conv + direct * gated[s].astype(jnp.float32)) * keep
        out[s] = total.astype(jnp.bfloat16)


def long_conv(gated, toeplitz, skip, shard_doc, live):
    shards, width, tok = gated.shape
    depth = toeplitz.shape[1]
    chans = min(CHANS, width)
    blocks = shards * tok // ROWS
    pairs = (depth // ROWS + 1) // 2
    tall = blocks + 8 * (pairs - 1)
    smem = pl.BlockSpec(memory_space=pltpu.SMEM)
    slab = pl.BlockSpec((shards, chans, tok), lambda i: (0, i, 0))
    return pl.pallas_call(
        conv_kernel,
        grid=(width // chans,),
        in_specs=[
            smem,
            smem,
            pl.BlockSpec((chans, 1), lambda i: (i, 0)),
            pl.BlockSpec((chans, depth, 4 * ROWS), lambda i: (i, 0, 0)),
            slab,
        ],
        out_specs=slab,
        out_shape=jax.ShapeDtypeStruct((shards, width, tok), jnp.bfloat16),
        scratch_shapes=[
            pltpu.VMEM((pairs + 1, blocks, LANES), jnp.bfloat16),
            pltpu.VMEM(((tall + 1) * (chans + 1), LANES), jnp.float32),
            pltpu.VMEM((UNROLL, tall, LANES), jnp.float32),
            pltpu.VMEM((UNROLL, blocks + 8, LANES), jnp.float32),
            pltpu.VMEM(((blocks + 1) * (chans + 1), LANES), jnp.float32),
        ],
        compiler_params=pltpu.CompilerParams(
            vmem_limit_bytes=VMEM, dimension_semantics=("arbitrary",)
        ),
        cost_estimate=pl.CostEstimate(flops=1, bytes_accessed=1, transcendentals=0),
        name="long_conv",
    )(shard_doc, live, skip, toeplitz, gated)


def gate_kernel(fars, *refs):
    blocks, conv, own, sent = refs[:-3], refs[-3], refs[-2], refs[-1]
    shards, _, tok = conv.shape
    halves = sent.shape[0] + 1
    per = shards // halves
    span = len(fars) // halves
    here = lax.axis_index("ctx")
    mine = lax.axis_index("ch")
    for far, block in zip(fars, blocks):
        chip = (here // CORES) ^ far
        first = chip * CORES
        away = (first // per + halves - mine) % halves
        values = [
            (block[k].astype(jnp.float32) * conv[first + k].astype(jnp.float32)).astype(
                jnp.bfloat16
            )
            for k in range(CORES)
        ]
        value = jnp.concatenate(values, axis=1)
        start = chip % span * (CORES * tok)
        column = pl.ds(pl.multiple_of(start, CORES * tok), CORES * tok)

        @pl.when(away == 0)
        def _():
            own[:, column] = value

        @pl.when(away != 0)
        def _():
            sent[away - 1, :, column] = value


def gate(fars, blocks, conv, halves):
    _, width, tok = blocks[0].shape
    shards = conv.shape[0]
    chans = min(64, width)
    wide = len(fars) // halves * CORES * tok
    return pl.pallas_call(
        functools.partial(gate_kernel, fars),
        grid=(width // chans,),
        in_specs=[pl.BlockSpec((CORES, chans, tok), lambda i: (0, i, 0))] * len(blocks)
        + [pl.BlockSpec((shards, chans, tok), lambda i: (0, i, 0))],
        out_specs=[
            pl.BlockSpec((chans, wide), lambda i: (i, 0)),
            pl.BlockSpec((halves - 1, chans, wide), lambda i: (0, i, 0)),
        ],
        out_shape=[
            jax.ShapeDtypeStruct((width, wide), jnp.bfloat16),
            jax.ShapeDtypeStruct((halves - 1, width, wide), jnp.bfloat16),
        ],
        compiler_params=pltpu.CompilerParams(vmem_limit_bytes=VMEM),
        cost_estimate=pl.CostEstimate(flops=1, bytes_accessed=1, transcendentals=0),
        name="gate",
    )(*blocks, conv)


def local(qkv, short_filter, long_filter, skip, shard_doc, live):
    shards = lax.axis_size("ctx")
    halves = lax.axis_size("ch")
    here = lax.axis_index("ctx")
    mine = lax.axis_index("ch")
    tok, width = qkv.shape[1:]
    part = width // shards
    chips = shards // CORES
    span = chips // halves
    border = lax.ppermute(
        qkv[:, tok - 2 :, :], "ctx", [(i, i + 1) for i in range(shards - 1)]
    )
    filt = lax.dynamic_slice_in_dim(long_filter, here * part, part, axis=1)
    direct = lax.dynamic_slice_in_dim(skip, here * part, part, axis=0)
    out = jnp.zeros((halves, part, shards * tok // halves), jnp.bfloat16)

    def across(block, distance):
        return lax.ppermute(block, "ctx", [(i, i ^ distance) for i in range(shards)])

    (gated,) = short_convs(qkv, short_filter, shard_doc, live, (1, 2), False)
    gated = first_tokens(gated, qkv, border, short_filter, shard_doc, live)
    qkv, gated = lax.optimization_barrier((qkv, gated))
    queries = short_convs(qkv, short_filter, shard_doc, live, (0,), True, border)
    gated = lax.all_to_all(gated, "ctx", 0, 0)
    queries = [queries[0]] + [across(queries[k], k) for k in range(1, CORES)]
    queries = pair_up(queries)
    cuts = [0, span // 4, span // 2, span * 3 // 4, span]
    groups = [
        [near + h * span for near in range(low, high) for h in reversed(range(halves))]
        for low, high in zip(cuts, cuts[1:])
    ]
    order = [far for fars in groups for far in fars if far]
    order = sorted(order, key=lambda far: far != 1)
    got = {0: queries[0]}

    def launch(fars, after):
        blocks, after = lax.optimization_barrier(([queries[far] for far in fars], after))
        for far, block in zip(fars, blocks):
            got[far] = across(block, far * CORES)
        return after

    early = [1, span, span - 1]
    for far in early:
        got[far] = across(queries[far], far * CORES)
    got[1], filt = lax.optimization_barrier((got[1], filt))
    toeplitz, direct = prepare(filt, direct)
    order = [far for far in order if far not in early]
    order = sorted(order, key=lambda far: (far not in groups[0] + groups[1], far < span))
    last = [far for far in order if far in groups[-1]]
    middle = [far for far in order if far not in last]
    late = last
    gated, toeplitz = launch(middle, (gated, toeplitz))
    got[1], gated = lax.optimization_barrier((got[1], gated))
    conv = long_conv(gated, toeplitz, direct, shard_doc, live)
    for fars in groups:
        own, sent = gate(fars, [got[far] for far in fars], conv, halves)
        if late:
            sent = launch(late, sent)
            late = []
        wide = own.shape[1]
        first = (here // CORES) % span ^ fars[-1]
        start = first // (len(fars) // halves) * wide
        out = lax.dynamic_update_slice(out, own[None], (mine, 0, start))
        for d in range(1, halves):
            route = [(j, (j + d) % halves) for j in range(halves)]
            came = lax.ppermute(sent[d - 1], "ch", route)
            source = lax.rem(mine + halves - d, halves)
            out = lax.dynamic_update_slice(out, came[None], (source, 0, start))
    return out


def solution(mesh):
    return jax.shard_map(
        local,
        mesh=mesh,
        in_specs=(P(None, "ctx", "ch"), P(None, None, "ch"), P(None, "ch"), P("ch"), P(), P()),
        out_specs=P(None, "ctx", "ch"),
        check_vma=False,
    )
```

```python
import functools

import jax
import jax.numpy as jnp
from jax import lax
from jax.experimental import pallas as pl
from jax.experimental.pallas import tpu as pltpu
from jax.sharding import PartitionSpec as P

LANES = 128
UNROLL = 32
ROWS = 64
CORES = 2
CHANS = 32
VMEM = 56 << 20


def shard_facts(doc, live, tok):
    shards = doc.shape[0]
    here = lax.axis_index("ctx")
    before = jnp.maximum(here - 1, 0)
    after = jnp.minimum(here + 1, shards - 1)
    joined = (here > 0) & (doc[before] == doc[here])
    closing = (here == shards - 1) | (doc[after] != doc[here])
    return joined, jnp.where(closing, live[here], tok)


def short_kernel(count, edges, doc, live, *refs):
    taps, slabs = refs[:count], refs[count : 2 * count]
    borders, refs = refs[2 * count : 2 * count + edges], refs[2 * count + edges :]
    outs, tall, turned = refs[:-2], refs[-2], refs[-1]
    here = lax.axis_index("ctx")
    tok = slabs[0].shape[1]
    joined, limit = shard_facts(doc, live, tok)

    def short(a):
        x = slabs[a][0].astype(jnp.float32)
        edge = jnp.zeros((2, x.shape[1]), jnp.float32)
        if edges:
            edge = jnp.where(joined, borders[a][0].astype(jnp.float32), 0.0)
        tall[a, 6:8, :] = edge
        tall[a, pl.ds(8, tok), :] = x
        once = tall[a, pl.ds(7, tok), :]
        twice = tall[a, pl.ds(6, tok), :]
        tap = taps[a]
        return tap[0, 0:1, :] * x + tap[0, 1:2, :] * once + tap[0, 2:3, :] * twice

    value = short(0)
    if count == 2:
        rows = lax.broadcasted_iota(jnp.int32, value.shape, 0)
        value = value * short(1) * jnp.where(rows < limit, 1.0, 0.0)
    value = value.astype(jnp.bfloat16).T
    if len(outs) == 1:
        part = outs[0].shape[1]
        for j in range(outs[0].shape[0]):
            outs[0][j] = value[j * part : (j + 1) * part]
    else:
        turned[...] = value
        part = outs[0].shape[1]
        for k, out in enumerate(outs):
            for j in range(out.shape[0]):
                row = (CORES * j + ((here % CORES) ^ k)) * part
                out[j] = turned[pl.ds(pl.multiple_of(row, part), part), :]


def short_convs(qkv, short_filter, shard_doc, live, which, split, border=None):
    _, tok, width = qkv.shape
    shards = shard_doc.shape[0]
    part = width // shards
    block = min(width, 512)
    smem = pl.BlockSpec(memory_space=pltpu.SMEM)
    count = len(which)
    borders = [] if border is None else [border] * count

    def spec(rows, a):
        return pl.BlockSpec((1, rows, block), lambda i: (a, 0, i))

    many = CORES if split else 1
    rows = block // part // many
    return pl.pallas_call(
        functools.partial(short_kernel, count, len(borders)),
        grid=(width // block,),
        in_specs=[smem] * 2
        + [spec(3, a) for a in which]
        + [spec(tok, a) for a in which]
        + [spec(2, a) for a in which if border is not None],
        out_specs=[pl.BlockSpec((rows, part, tok), lambda i: (i, 0, 0))] * many,
        out_shape=[jax.ShapeDtypeStruct((shards // many, part, tok), jnp.bfloat16)] * many,
        scratch_shapes=[
            pltpu.VMEM((count, tok + 8, block), jnp.float32),
            pltpu.VMEM((block, tok), jnp.bfloat16),
        ],
        compiler_params=pltpu.CompilerParams(vmem_limit_bytes=VMEM),
        name="short_" + "".join("qkv"[a] for a in which),
    )(shard_doc, live, *[short_filter] * count, *[qkv] * count, *borders)


def first_kernel(doc, live, key_edge, value_edge, key_taps, value_taps, key, value, old, out):
    shards, part, _ = old.shape
    tok = 2
    joined, limit = shard_facts(doc, live, tok)

    def short(edge, taps, slab):
        x = slab[0, :tok, :].astype(jnp.float32)
        edge = jnp.where(joined, edge[0].astype(jnp.float32), 0.0)
        once = jnp.concatenate([edge[1:], x[:1]], axis=0)
        return taps[0, 0:1, :] * x + taps[0, 1:2, :] * once + taps[0, 2:3, :] * edge

    keep = jnp.where(lax.broadcasted_iota(jnp.int32, (tok, 1), 0) < limit, 1.0, 0.0)
    both = short(key_edge, key_taps, key) * short(value_edge, value_taps, value) * keep
    tall = jnp.concatenate([both, jnp.zeros((LANES - tok, both.shape[1]), jnp.float32)], axis=0)
    new = tall.astype(jnp.bfloat16).T.reshape(shards, part, LANES)
    place = lax.broadcasted_iota(jnp.int32, new.shape, 2)
    out[...] = jnp.where(place < tok, new, old[...])


def first_tokens(gated, qkv, border, short_filter, shard_doc, live):
    shards, part, _ = gated.shape
    width = shards * part
    smem = pl.BlockSpec(memory_space=pltpu.SMEM)

    def spec(rows, a):
        return pl.BlockSpec((1, rows, width), lambda i: (a, 0, 0))

    tile = pl.BlockSpec((shards, part, LANES), lambda i: (0, 0, 0))
    return pl.pallas_call(
        first_kernel,
        grid=(1,),
        in_specs=[smem] * 2 + [spec(rows, a) for rows in (2, 3, 16) for a in (1, 2)] + [tile],
        out_specs=tile,
        out_shape=jax.ShapeDtypeStruct(gated.shape, gated.dtype),
        input_output_aliases={8: 0},
        compiler_params=pltpu.CompilerParams(vmem_limit_bytes=VMEM),
        name="first_tokens",
    )(shard_doc, live, *[border] * 2, *[short_filter] * 2, *[qkv] * 2, gated)


def pair_up_kernel(*refs):
    blocks, outs = refs[:CORES], refs[CORES:]
    here = lax.axis_index("ctx")
    for k, block in enumerate(blocks):
        row = (here % CORES) ^ k
        for far, out in enumerate(outs):
            out[row] = block[(here // CORES) ^ far]


def pair_up(blocks):
    chips, part, tok = blocks[0].shape
    vmem = pl.BlockSpec(memory_space=pltpu.VMEM)
    return pl.pallas_call(
        pair_up_kernel,
        in_specs=[vmem] * CORES,
        out_specs=[vmem] * chips,
        out_shape=[jax.ShapeDtypeStruct((CORES, part, tok), jnp.bfloat16)] * chips,
        compiler_params=pltpu.CompilerParams(vmem_limit_bytes=VMEM),
        name="pair_up",
    )(*blocks)


def prepare_kernel(filt, skip, out, column, taps):
    step = pl.program_id(0)
    chans, rows, width = out.shape

    @pl.when(step == 0)
    def _():
        taps[...] = filt[...].astype(jnp.float32).T

        column[...] = jnp.broadcast_to(skip[...], (8, skip.shape[1])).T[:, :1]

    def channel(c, _):
        row = taps[pl.ds(step * chans + c, 1), :]
        row = jnp.concatenate([row, jnp.zeros((1, width), jnp.float32)], axis=1)
        spread = jnp.broadcast_to(row, (16, row.shape[1]))
        band = pltpu.roll(spread, 0, 1, stride=1, stride_axis=0).astype(jnp.bfloat16)
        bands = [band] + [pltpu.roll(band, 16 * q, 1) for q in range(1, ROWS // 16)]
        toeplitz = jnp.concatenate(bands, axis=0)
        for k in range(rows // ROWS):
            out[c, k * ROWS : (k + 1) * ROWS, :] = toeplitz[:, k * width : (k + 1) * width]
        return 0

    lax.fori_loop(0, chans, channel, 0, unroll=8)


def prepare(filt, skip):
    lags, part = filt.shape
    chans = min(CHANS, part)
    width = 4 * ROWS
    rows = (lags // width + 1) * ROWS
    return pl.pallas_call(
        prepare_kernel,
        grid=(part // chans,),
        in_specs=[
            pl.BlockSpec((lags, part), lambda i: (0, 0)),
            pl.BlockSpec((1, part), lambda i: (0, 0)),
        ],
        out_specs=[
            pl.BlockSpec((chans, rows, width), lambda i: (i, 0, 0)),
            pl.BlockSpec((part, 1), lambda i: (0, 0)),
        ],
        out_shape=[
            jax.ShapeDtypeStruct((part, rows, width), jnp.bfloat16),
            jax.ShapeDtypeStruct((part, 1), jnp.float32),
        ],
        scratch_shapes=[pltpu.VMEM((part, lags), jnp.float32)],
        compiler_params=pltpu.CompilerParams(
            vmem_limit_bytes=VMEM, dimension_semantics=("arbitrary",)
        ),
        name="prepare",
    )(filt, skip[None, :])


def conv_kernel(doc, live, skip, toeplitz, gated, out, masks, wide, one, late, mixed):
    shards, chans, tok = gated.shape
    pitch = chans + 1
    per = tok // LANES
    fine = tok // ROWS
    blocks = shards * fine
    pairs = masks.shape[0] - 1
    pad = 8 * (pairs - 1)
    step = pl.program_id(0)
    depth = toeplitz.shape[1]

    @pl.when(step == 0)
    def _():
        wide[pl.ds(0, pad * pitch), :] = jnp.zeros((pad * pitch, LANES), jnp.float32)
        late[:, pl.ds(0, 8), :] = jnp.zeros((late.shape[0], 8, LANES), jnp.float32)
        start = jnp.int32(0)
        rows = lax.broadcasted_iota(jnp.int32, (fine, LANES), 0)
        left = lax.broadcasted_iota(jnp.int32, (blocks, LANES), 1) < ROWS
        runs = []
        for s in range(shards):
            if s > 0:
                start = jnp.where(doc[s] == doc[s - 1], start, s)
            runs.append(rows + (s - start) * fine)
        run = jnp.concatenate(runs, axis=0)
        for m in range(pairs):
            reach = jnp.where(left, 8 * m, 8 * m + 4)
            masks[m] = jnp.where(run >= reach, 1.0, 0.0).astype(jnp.bfloat16)
        masks[pairs] = jnp.where(run >= 2, 1.0, 0.0).astype(jnp.bfloat16)

    left = lax.broadcasted_iota(jnp.int32, (chans, LANES), 1) < ROWS
    older = [(jnp.zeros((chans, LANES), jnp.float32),) * 2] * 2
    for s in range(shards):
        for b in range(per):
            here = gated[s, :, b * LANES : (b + 1) * LANES].astype(jnp.float32)
            turned = pltpu.roll(here, ROWS, 1)
            row = pad + s * fine + 2 * b
            wide[pl.ds(row * pitch, chans), :] = jnp.where(left, here, older[0][1])
            wide[pl.ds((row + 1) * pitch, chans), :] = jnp.where(left, turned, older[0][0])
            older = [older[1], (here, turned)]

    def channel(c, slot):
        one[slot] = wide[pl.ds(c, blocks + pad, stride=pitch), :]
        lagged = [
            one[slot, pl.ds(pad - 8 * m, blocks), :].astype(jnp.bfloat16) * masks[m]
            for m in range(pairs)
        ]
        sums = jnp.dot(
            jnp.concatenate(lagged, axis=1)[:, :depth],
            toeplitz[c],
            preferred_element_type=jnp.float32,
        )
        late[slot, pl.ds(8, blocks), :] = sums[:, LANES:]
        behind = late[slot, pl.ds(6, blocks), :] * masks[pairs].astype(jnp.float32)
        mixed[pl.ds(c, blocks, stride=pitch), :] = sums[:, :LANES] + behind

    def group(i, _):
        for slot in range(UNROLL):
            channel(i * UNROLL + slot, slot)
        return 0

    lax.fori_loop(0, chans // UNROLL, group, 0)

    direct = skip[...]
    places = lax.broadcasted_iota(jnp.int32, (1, tok), 1)
    for s in range(shards):
        if s < shards - 1:
            limit = jnp.where(doc[s] != doc[s + 1], live[s], tok)
        else:
            limit = live[s]
        keep = jnp.where(places < limit, 1.0, 0.0)
        sums = []
        for b in range(per):
            row = s * fine + 2 * b
            after = mixed[pl.ds((row + 1) * pitch, chans), :]
            if row > 0:
                spill = mixed[pl.ds((row - 1) * pitch, chans), :]
                if b == 0:
                    spill = jnp.where(doc[s] == doc[s - 1], spill, 0.0)
            else:
                spill = jnp.zeros_like(after)
            sums.append(
                mixed[pl.ds(row * pitch, chans), :]
                + pltpu.roll(jnp.where(left, after, spill), ROWS, 1)
            )
        conv = jnp.concatenate(sums, axis=1)
        total = (conv + direct * gated[s].astype(jnp.float32)) * keep
        out[s] = total.astype(jnp.bfloat16)


def long_conv(gated, toeplitz, skip, shard_doc, live):
    shards, width, tok = gated.shape
    depth = toeplitz.shape[1]
    chans = min(CHANS, width)
    blocks = shards * tok // ROWS
    pairs = (depth // ROWS + 1) // 2
    tall = blocks + 8 * (pairs - 1)
    smem = pl.BlockSpec(memory_space=pltpu.SMEM)
    slab = pl.BlockSpec((shards, chans, tok), lambda i: (0, i, 0))
    return pl.pallas_call(
        conv_kernel,
        grid=(width // chans,),
        in_specs=[
            smem,
            smem,
            pl.BlockSpec((chans, 1), lambda i: (i, 0)),
            pl.BlockSpec((chans, depth, 4 * ROWS), lambda i: (i, 0, 0)),
            slab,
        ],
        out_specs=slab,
        out_shape=jax.ShapeDtypeStruct((shards, width, tok), jnp.bfloat16),
        scratch_shapes=[
            pltpu.VMEM((pairs + 1, blocks, LANES), jnp.bfloat16),
            pltpu.VMEM(((tall + 1) * (chans + 1), LANES), jnp.float32),
            pltpu.VMEM((UNROLL, tall, LANES), jnp.float32),
            pltpu.VMEM((UNROLL, blocks + 8, LANES), jnp.float32),
            pltpu.VMEM(((blocks + 1) * (chans + 1), LANES), jnp.float32),
        ],
        compiler_params=pltpu.CompilerParams(
            vmem_limit_bytes=VMEM, dimension_semantics=("arbitrary",)
        ),
        cost_estimate=pl.CostEstimate(flops=1, bytes_accessed=1, transcendentals=0),
        name="long_conv",
    )(shard_doc, live, skip, toeplitz, gated)


def gate_kernel(fars, *refs):
    blocks, conv, own, sent = refs[:-3], refs[-3], refs[-2], refs[-1]
    shards, _, tok = conv.shape
    halves = sent.shape[0] + 1
    per = shards // halves
    span = len(fars) // halves
    here = lax.axis_index("ctx")
    mine = lax.axis_index("ch")
    for far, block in zip(fars, blocks):
        chip = (here // CORES) ^ far
        first = chip * CORES
        away = (first // per + halves - mine) % halves
        values = [
            (block[k].astype(jnp.float32) * conv[first + k].astype(jnp.float32)).astype(
                jnp.bfloat16
            )
            for k in range(CORES)
        ]
        value = jnp.concatenate(values, axis=1)
        start = chip % span * (CORES * tok)
        column = pl.ds(pl.multiple_of(start, CORES * tok), CORES * tok)

        @pl.when(away == 0)
        def _():
            own[:, column] = value

        @pl.when(away != 0)
        def _():
            sent[away - 1, :, column] = value


def gate(fars, blocks, conv, halves):
    _, width, tok = blocks[0].shape
    shards = conv.shape[0]
    chans = min(64, width)
    wide = len(fars) // halves * CORES * tok
    return pl.pallas_call(
        functools.partial(gate_kernel, fars),
        grid=(width // chans,),
        in_specs=[pl.BlockSpec((CORES, chans, tok), lambda i: (0, i, 0))] * len(blocks)
        + [pl.BlockSpec((shards, chans, tok), lambda i: (0, i, 0))],
        out_specs=[
            pl.BlockSpec((chans, wide), lambda i: (i, 0)),
            pl.BlockSpec((halves - 1, chans, wide), lambda i: (0, i, 0)),
        ],
        out_shape=[
            jax.ShapeDtypeStruct((width, wide), jnp.bfloat16),
            jax.ShapeDtypeStruct((halves - 1, width, wide), jnp.bfloat16),
        ],
        compiler_params=pltpu.CompilerParams(vmem_limit_bytes=VMEM),
        cost_estimate=pl.CostEstimate(flops=1, bytes_accessed=1, transcendentals=0),
        name="gate",
    )(*blocks, conv)


def local(qkv, short_filter, long_filter, skip, shard_doc, live):
    shards = lax.axis_size("ctx")
    halves = lax.axis_size("ch")
    here = lax.axis_index("ctx")
    mine = lax.axis_index("ch")
    tok, width = qkv.shape[1:]
    part = width // shards
    chips = shards // CORES
    span = chips // halves
    border = lax.ppermute(
        qkv[:, tok - 2 :, :], "ctx", [(i, i + 1) for i in range(shards - 1)]
    )
    filt = lax.dynamic_slice_in_dim(long_filter, here * part, part, axis=1)
    direct = lax.dynamic_slice_in_dim(skip, here * part, part, axis=0)
    out = jnp.zeros((halves, part, shards * tok // halves), jnp.bfloat16)

    def across(block, distance):
        return lax.ppermute(block, "ctx", [(i, i ^ distance) for i in range(shards)])

    (gated,) = short_convs(qkv, short_filter, shard_doc, live, (1, 2), False)
    gated = first_tokens(gated, qkv, border, short_filter, shard_doc, live)
    qkv, gated = lax.optimization_barrier((qkv, gated))
    queries = short_convs(qkv, short_filter, shard_doc, live, (0,), True, border)
    gated = lax.all_to_all(gated, "ctx", 0, 0)
    queries = [queries[0]] + [across(queries[k], k) for k in range(1, CORES)]
    queries = pair_up(queries)
    cuts = [0, span // 4, span // 2, span * 3 // 4, span]
    groups = [
        [near + h * span for near in range(low, high) for h in reversed(range(halves))]
        for low, high in zip(cuts, cuts[1:])
    ]
    order = [far for fars in groups for far in fars if far]
    order = sorted(order, key=lambda far: far != 1)
    got = {0: queries[0]}

    def launch(fars, after):
        blocks, after = lax.optimization_barrier(([queries[far] for far in fars], after))
        for far, block in zip(fars, blocks):
            got[far] = across(block, far * CORES)
        return after

    early = [1, span, span - 1]
    for far in early:
        got[far] = across(queries[far], far * CORES)
    got[1], filt = lax.optimization_barrier((got[1], filt))
    toeplitz, direct = prepare(filt, direct)
    order = [far for far in order if far not in early]
    order = sorted(order, key=lambda far: (far not in groups[0] + groups[1], far < span))
    last = [far for far in order if far in groups[-1]]
    middle = [far for far in order if far not in last]
    late = last
    gated, toeplitz = launch(middle, (gated, toeplitz))
    got[1], gated = lax.optimization_barrier((got[1], gated))
    conv = long_conv(gated, toeplitz, direct, shard_doc, live)
    for fars in groups:
        own, sent = gate(fars, [got[far] for far in fars], conv, halves)
        if late:
            sent = launch(late, sent)
            late = []
        wide = own.shape[1]
        first = (here // CORES) % span ^ fars[-1]
        start = first // (len(fars) // halves) * wide
        out = lax.dynamic_update_slice(out, own[None], (mine, 0, start))
        for d in range(1, halves):
            route = [(j, (j + d) % halves) for j in range(halves)]
            came = lax.ppermute(sent[d - 1], "ch", route)
            source = lax.rem(mine + halves - d, halves)
            out = lax.dynamic_update_slice(out, came[None], (source, 0, start))
    return out


def solution(mesh):
    return jax.shard_map(
        local,
        mesh=mesh,
        in_specs=(P(None, "ctx", "ch"), P(None, None, "ch"), P(None, "ch"), P("ch"), P(), P()),
        out_specs=P(None, "ctx", "ch"),
        check_vma=False,
    )
```
